128 devices in a mesh: row: 16 (over x, y), col: 8 (over z, core).
Axes of the slice: x: 4, y: 4, z: 4, core: 2. Of those that a mesh axis runs over, the one named last changes fastest.
Arguments:
- pair: bfloat16 [640, 640, 128], P('row', 'col'), may hold values from -6 to 6
- pair_mask: int32 [640, 640], P('row', 'col'), may hold values 0 or 1
- node_state: float32 [640, 64], P('row'), may hold values from -6 to 6
- coords: float32 [3, 640], P(None, 'row'), may hold values from -40 to 40
- neighbours: int32 [640, 64], P('row'), may hold values from 0 to 639
- atom_type: int32 [640], P('row'), may hold values from 0 to 79
- type_table: float32 [80, 64], replicated, may hold values from -4 to 4
- node_query: float32 [64, 64], replicated, may hold values from -0.75 to 0.75
- node_key: float32 [64, 64], replicated, may hold values from -0.75 to 0.75
- node_value: float32 [64, 64], replicated, may hold values from -0.75 to 0.75
- edge_pair: bfloat16 [128, 128], replicated, may hold values from -0.5 to 0.5
- edge_radial: float32 [64, 128], replicated, may hold values from -4 to 49
- node_out_w: float32 [64, 64], replicated, may hold values from -0.75 to 0.75
- coord_gain: float32 [4], replicated, may hold values from 0.02 to 0.12
- radial_pair: float32 [64, 128], replicated, may hold values from -4 to 4
- row_gain: float32 [128], replicated, may hold values from 0.5 to 1.5
- row_query: bfloat16 [128, 128], replicated, may hold values from -1 to 1
- row_key: bfloat16 [128, 128], replicated, may hold values from -1 to 1
- row_value: bfloat16 [128, 128], replicated, may hold values from -1.75 to 1.75
- row_gate: bfloat16 [128, 128], replicated, may hold values from -0.5 to 0.5
- row_out: bfloat16 [128, 128], replicated, may hold values from -1.75 to 1.75
- row_bias: float32 [64, 4], replicated, may hold values from -8 to 143
- column_gain: float32 [128], replicated, may hold values from 0.5 to 1.5
- column_query: bfloat16 [128, 128], replicated, may hold values from -1 to 1
- column_key: bfloat16 [128, 128], replicated, may hold values from -1 to 1
- column_value: bfloat16 [128, 128], replicated, may hold values from -1 to 1
- column_gate: bfloat16 [128, 128], replicated, may hold values from -0.5 to 0.5
- column_out: bfloat16 [128, 128], replicated, may hold values from -1 to 1
- column_bias: float32 [64, 4], replicated, may hold values from -8 to 143
Outputs:
- pair_out: bfloat16 [640, 640, 128], P('row', 'col')
- node_out: float32 [640, 64], P('row')
- coords_out: float32 [3, 640], P(None, 'row')
The draws below stay inside these ranges and needn't reach their ends.
Inputs may be any that keep to these rules, and one draw needn't show every extreme that they name: `neighbours`: token indices. `atom_type`: type indices.
All inputs are finite; a program needn't handle non-finite values. No bound on the sum of `pair_mask` on one device may be relied on, other than what follows from the above.
Results may differ from the reference program's by a relative error of at most 0.034.
Values may be sent and summed in bfloat16 or wider, within the bound.
No kernel may reach another device: no remote copies, remote signals or barrier semaphores. Data moves between devices by JAX's collectives and lax.ppermute only.
A program may use at most 128 MiB of HBM per device.

```python
import math
import jax
import jax.numpy as jnp
from jax import lax

L = 640
CP = 128
PHEADS = 4
CN = 64
GHEADS = 4
NEIGH = 64
NB = 64
NTYPE = 80


def bias_levels(key, bins, heads):
    noise_key = jax.random.fold_in(key, 0)
    noise = 2.0 * jnp.clip(jax.random.normal(noise_key, (bins, heads), jnp.float32), -4.0, 4.0)
    return noise


def radial_table(key, bins, width):
    noise = 0.6 * jnp.clip(jax.random.normal(key, (bins, 2 * width), jnp.float32), -6.0, 6.0)
    return noise


def draw_row_bias(key, part):
    key = jax.random.fold_in(key, 21)
    return bias_levels(key, NB, PHEADS)


def draw_column_bias(key, part):
    key = jax.random.fold_in(key, 22)
    return bias_levels(key, NB, PHEADS)


def draw_edge_radial(key, part):
    key = jax.random.fold_in(key, 23)
    return radial_table(key, NB, CN)


def touch_ends(entries, rng, low, high):
    longest = entries.shape.index(max(entries.shape))
    spots = []
    for shift in (0, 1):
        where = [jax.random.randint(jax.random.fold_in(rng, axis), (), 0, length) for axis, length in enumerate(entries.shape)]
        where[longest] = (where[longest] + shift) % entries.shape[longest]
        spots.append(tuple(where))
    return entries.at[spots[0]].set(low).at[spots[1]].set(high)


def steps_of(stream_key, shape, cuts, smallest, largest):
    gain = 1.0
    for axis_at, shards_of in cuts:
        heights = jax.random.uniform(jax.random.fold_in(jax.random.fold_in(stream_key, 6), axis_at), (shards_of,), jnp.float32, smallest / len(cuts), largest / len(cuts))
        gain = gain * jnp.repeat(jnp.exp(heights), shape[axis_at] // shards_of).reshape((-1,) + (1,) * (len(shape) - 1 - axis_at))
    return gain


def scatter_about(stream_key, shape, scale, most, pieces=(), kind=jnp.bfloat16):
    entries = jax.random.normal(stream_key, shape, jnp.float32) * scale
    if len(pieces) > 0:
        entries = steps_of(stream_key, shape, pieces, -0.22, 0.18) * entries
    return jnp.clip(entries, min=-most, max=most).astype(kind)


def setup_inputs(seed: int = 0) -> dict:
    splits = jax.random.split(jax.random.key(seed), 30)
    return {
        "pair": scatter_about(splits[0], (L, L, CP), 1.0, 6.0, ((0, 16), (1, 8))),
        "pair_mask": touch_ends((jax.random.randint(splits[1], (L, L), 0, 8) < 7).astype(jnp.int32), jax.random.fold_in(splits[1], 1), 0, 1),
        "node_state": scatter_about(splits[2], (L, CN), 1.0, 6.0, ((0, 16),), jnp.float32),
        "coords": scatter_about(splits[3], (3, L), 8.0, 40.0, ((1, 16),), jnp.float32),
        "neighbours": touch_ends(jax.random.randint(splits[4], (L, NEIGH), 0, L), jax.random.fold_in(splits[4], 1), 0, L - 1).astype(jnp.int32),
        "atom_type": touch_ends(jax.random.randint(splits[5], (L,), 0, NTYPE), jax.random.fold_in(splits[5], 1), 0, NTYPE - 1).astype(jnp.int32),
        "type_table": scatter_about(splits[6], (NTYPE, CN), 0.7, 4.0, (), jnp.float32),
        "node_query": scatter_about(splits[7], (CN, CN), CN ** -0.5, 0.75, (), jnp.float32),
        "node_key": scatter_about(splits[8], (CN, CN), CN ** -0.5, 0.75, (), jnp.float32),
        "node_value": scatter_about(splits[9], (CN, CN), CN ** -0.5, 0.75, (), jnp.float32),
        "edge_pair": scatter_about(splits[10], (CP, 2 * CN), CP ** -0.5, 0.5),
        "edge_radial": draw_edge_radial(jax.random.fold_in(splits[29], 71), 0),
        "node_out_w": scatter_about(splits[12], (CN, CN), CN ** -0.5, 0.75, (), jnp.float32),
        "coord_gain": jnp.clip(jax.random.uniform(splits[13], (GHEADS,), jnp.float32, 0.02, 0.12), 0.02, 0.12),
        "radial_pair": scatter_about(splits[14], (NB, CP), 0.6, 4.0, (), jnp.float32),
        "row_gain": jnp.clip(1.0 + 0.1 * jax.random.normal(splits[15], (CP,), jnp.float32), 0.5, 1.5),
        "row_query": scatter_about(splits[16], (CP, CP), (CP // 4) ** -0.5, 1.0),
        "row_key": scatter_about(splits[17], (CP, CP), (CP // 4) ** -0.5, 1.0),
        "row_value": scatter_about(splits[18], (CP, CP), 11 ** -0.5, 1.75),
        "row_gate": scatter_about(splits[19], (CP, CP), CP ** -0.5, 0.5),
        "row_out": scatter_about(splits[20], (CP, CP), 11 ** -0.5, 1.75),
        "row_bias": draw_row_bias(jax.random.fold_in(splits[29], 71), 0),
        "column_gain": jnp.clip(1.0 + 0.1 * jax.random.normal(splits[22], (CP,), jnp.float32), 0.5, 1.5),
        "column_query": scatter_about(splits[23], (CP, CP), (CP // 4) ** -0.5, 1.0),
        "column_key": scatter_about(splits[24], (CP, CP), (CP // 4) ** -0.5, 1.0),
        "column_value": scatter_about(splits[25], (CP, CP), 32 ** -0.5, 1.0),
        "column_gate": scatter_about(splits[26], (CP, CP), CP ** -0.5, 0.5),
        "column_out": scatter_about(splits[27], (CP, CP), 32 ** -0.5, 1.0),
        "column_bias": draw_column_bias(jax.random.fold_in(splits[29], 71), 0),
    }


PRECISE = lax.Precision.HIGHEST
RADIAL_REACH = 24.0

def radial(spacing, bins):
    centers = jnp.arange(bins, dtype=jnp.float32) * (RADIAL_REACH / (bins - 1))
    spread_width = RADIAL_REACH / bins
    return jnp.exp(-jnp.square((spacing[..., None] - centers) / spread_width))

def distances(near_xyz, far_xyz):
    displacement = near_xyz[:, :, None] - far_xyz[:, None, :]
    return jnp.sqrt(lax.optimization_barrier(jnp.sum(displacement * displacement, axis=0)) + 1e-06)

def pair_bias(near_xyz, far_xyz, weight_bias):
    far_count = far_xyz.shape[1]
    block_size = math.gcd(far_count, 128)
    blocks = far_xyz.reshape(3, far_count // block_size, block_size).transpose(1, 0, 2)

    def one_block(column_xyz):
        features = radial(distances(near_xyz, column_xyz), weight_bias.shape[0])
        return jnp.einsum('abr,rh->hab', features, weight_bias, precision=PRECISE)
    stacked = lax.map(one_block, blocks)
    return stacked.transpose(1, 2, 0, 3).reshape(weight_bias.shape[1], near_xyz.shape[1], far_count)

def layer_norm(values, norm_gain):
    values = values.astype(jnp.float32)
    center = lax.optimization_barrier(jnp.mean(values, axis=-1, keepdims=True))
    spread = lax.optimization_barrier(jnp.mean(jnp.square(values - center), axis=-1, keepdims=True))
    return (values - center) * lax.rsqrt(spread + 1e-05) * norm_gain

def softmax_last(logits):
    highest = lax.optimization_barrier(jnp.max(logits, axis=-1, keepdims=True))
    scaled = jnp.exp(logits - highest)
    return scaled / lax.optimization_barrier(jnp.sum(scaled, axis=-1, keepdims=True))

def project_pair(pair_block, mask_block, length, norm_gain, w_query, w_key, w_value, w_gate, head_count):
    rows_n, cols_n, channels = pair_block.shape
    normed = layer_norm(pair_block, norm_gain).astype(jnp.bfloat16).reshape(rows_n * cols_n, channels)
    mask_cells = mask_block.astype(jnp.float32)[:, :, None]
    head_size = channels // head_count

    def linear(weight):
        return jnp.dot(normed, weight, preferred_element_type=jnp.float32).reshape(rows_n, cols_n, channels)
    query_rows = (linear(w_query) * mask_cells * (1.0 / math.sqrt(head_size))).astype(jnp.bfloat16)
    key_rows = (linear(w_key) * mask_cells * (1.0 / math.sqrt(length))).astype(jnp.bfloat16)
    value_rows = linear(w_value).astype(jnp.bfloat16)
    gate_values = jax.nn.sigmoid(linear(w_gate))
    return (query_rows, key_rows, value_rows, gate_values)

def finish_pass(pair_block, gate_values, mixed_heads, w_out):
    rows_n, cols_n, channels = pair_block.shape
    gated_rows = (gate_values * mixed_heads.reshape(rows_n, cols_n, channels)).astype(jnp.bfloat16)
    update = jnp.dot(gated_rows.reshape(rows_n * cols_n, channels), w_out, preferred_element_type=jnp.float32)
    return (pair_block.astype(jnp.float32) + update.reshape(rows_n, cols_n, channels)).astype(jnp.bfloat16)

def axial_tied(pair_block, mask_block, coord_xyz, norm_gain, w_query, w_key, w_value, w_gate, w_out, w_bias):
    rows_n, cols_n, channels = pair_block.shape
    head_count = w_bias.shape[1]
    query_rows, key_rows, value_rows, gate_values = project_pair(pair_block, mask_block, rows_n, norm_gain, w_query, w_key, w_value, w_gate, head_count)
    shaped = (rows_n, cols_n, head_count, channels // head_count)
    logits = jnp.einsum('njhd,nkhd->hjk', query_rows.astype(jnp.float32).reshape(shaped), key_rows.astype(jnp.float32).reshape(shaped))
    logits = logits + pair_bias(coord_xyz, coord_xyz, w_bias)
    weights = softmax_last(logits).astype(jnp.bfloat16)
    mixed_heads = jnp.einsum('hjk,nkhd->njhd', weights.astype(jnp.float32), value_rows.astype(jnp.float32).reshape(shaped))
    return finish_pass(pair_block, gate_values, mixed_heads, w_out)

def node_features(node_state, atom_type, type_table):
    onehot = (atom_type[:, None] == jnp.arange(type_table.shape[0], dtype=jnp.int32)[None, :]).astype(jnp.float32)
    return node_state + jnp.dot(onehot, type_table, precision=PRECISE)

def edge_projection(pair_rows, spacing, edge_pair, edge_radial):
    rows_n, neighbour_count, channels = pair_rows.shape
    from_pair = jnp.dot(pair_rows.reshape(rows_n * neighbour_count, channels), edge_pair, preferred_element_type=jnp.float32)
    basis = radial(spacing, edge_radial.shape[0]).reshape(rows_n * neighbour_count, edge_radial.shape[0])
    from_radial = jnp.dot(basis, edge_radial, precision=PRECISE)
    return (from_pair + from_radial).reshape(rows_n, neighbour_count, edge_pair.shape[1])

def node_update(pair, node_state, coords, neighbours, atom_type, type_table, node_query, node_key, node_value, edge_pair, edge_radial, node_out_w, coord_gain):
    node_count, channels = node_state.shape
    head_count = coord_gain.shape[0]
    head_size = channels // head_count
    neighbour_count = neighbours.shape[1]
    features = node_features(node_state, atom_type, type_table)
    query_rows = jnp.dot(features, node_query, precision=PRECISE).reshape(node_count, head_count, head_size)
    node_keys = jnp.dot(features, node_key, precision=PRECISE)
    node_values = jnp.dot(features, node_value, precision=PRECISE)
    pair_rows = pair[jnp.arange(node_count)[:, None], neighbours]
    offsets = coords[:, neighbours] - coords[:, :, None]
    spacing = jnp.sqrt(lax.optimization_barrier(jnp.sum(offsets * offsets, axis=0)) + 1e-06)
    edge_terms = edge_projection(pair_rows, spacing, edge_pair, edge_radial)
    shaped = (node_count, neighbour_count, head_count, head_size)
    key_rows = (node_keys[neighbours] + edge_terms[:, :, :channels]).reshape(shaped)
    value_rows = (node_values[neighbours] + edge_terms[:, :, channels:]).reshape(shaped)
    scores = lax.optimization_barrier(jnp.sum(query_rows[:, None] * key_rows, axis=-1)) * (1.0 / math.sqrt(head_size))
    highest = lax.optimization_barrier(jnp.max(scores, axis=1))
    scaled = jnp.exp(scores - highest[:, None])
    weight_total = lax.optimization_barrier(jnp.sum(scaled, axis=1))
    weighted = jnp.einsum('nkh,nkhd->nhd', scaled, value_rows, precision=PRECISE)
    shift_sum = jnp.einsum('nkh,cnk->cnh', scaled, offsets, precision=PRECISE)
    attended = (weighted / weight_total[:, :, None]).reshape(node_count, channels)
    new_state = features + jnp.dot(attended, node_out_w, precision=PRECISE)
    new_coords = coords + lax.optimization_barrier(jnp.sum(coord_gain[None, None, :] * shift_sum / weight_total[None], axis=2))
    return (new_state, new_coords)

def reference(pair, pair_mask, node_state, coords, neighbours, atom_type, type_table, node_query, node_key, node_value, edge_pair, edge_radial, node_out_w, coord_gain, radial_pair, row_gain, row_query, row_key, row_value, row_gate, row_out, row_bias, column_gain, column_query, column_key, column_value, column_gate, column_out, column_bias):
    new_state, new_coords = node_update(pair, node_state, coords, neighbours, atom_type, type_table, node_query, node_key, node_value, edge_pair, edge_radial, node_out_w, coord_gain)
    length, channels = (pair.shape[0], pair.shape[2])
    basis = radial(distances(new_coords, new_coords), radial_pair.shape[0])
    added = jnp.dot(basis.reshape(length * length, radial_pair.shape[0]), radial_pair, precision=PRECISE)
    pair_rbf = (pair.astype(jnp.float32) + added.reshape(length, length, channels)).astype(jnp.bfloat16)
    after_rows = axial_tied(pair_rbf, pair_mask, new_coords, row_gain, row_query, row_key, row_value, row_gate, row_out, row_bias)
    turned = axial_tied(jnp.swapaxes(after_rows, 0, 1), jnp.swapaxes(pair_mask, 0, 1), new_coords, column_gain, column_query, column_key, column_value, column_gate, column_out, column_bias)
    return (jnp.swapaxes(turned, 0, 1), new_state, new_coords)
```

```python
import functools
import math

import jax
import jax.numpy as jnp
from jax import lax
from jax.experimental import pallas as pl
from jax.experimental.pallas import tpu as pltpu
from jax.sharding import Mesh
from jax.sharding import PartitionSpec as P

BF16 = jnp.bfloat16
F32 = jnp.float32
PRECISE = lax.Precision.HIGHEST
RADIAL_REACH = 24.0
NEGATIVE = -1e30
EVERYWHERE = ("x", "y", "z", "core")

VMEM = pl.BlockSpec(memory_space=pltpu.VMEM)
SMEM = pl.BlockSpec(memory_space=pltpu.SMEM)
PARAMS = pltpu.CompilerParams(vmem_limit_bytes=44 * 1024 * 1024)

ROWS, COLS, CH, HEADS = 40, 80, 128, 4
LENGTH = 640
LANES = 128
SLOT = 32
BLOCK = 32
OWNERS = 10
HALF = LENGTH // 2


def call(kernel, out_shape, in_specs, scratch=(), cost=None, out_specs=None):
    if out_specs is None:
        out_specs = jax.tree.map(lambda _: VMEM, out_shape)
    return pl.pallas_call(
        kernel,
        out_shape=out_shape,
        in_specs=in_specs,
        out_specs=out_specs,
        scratch_shapes=list(scratch),
        compiler_params=PARAMS,
        cost_estimate=cost,
    )


def shape(dims, dtype):
    return jax.ShapeDtypeStruct(dims, dtype)


def iota(dims, axis):
    return lax.broadcasted_iota(jnp.int32, dims, axis)


def dot(a, b):
    return jnp.dot(a, b, preferred_element_type=F32)


def dot32(a, b):
    return jnp.dot(a, b, preferred_element_type=F32, precision=PRECISE)


def split(a):
    high = a.astype(BF16)
    return high, (a - high.astype(F32)).astype(BF16)


def graph_kernel(
    start_ref, xyz_ref, pair_ref, near_ref, far_ref, neigh_ref, wq_ref, wkv_ref, ep_ref, er_ref,
    out_ref, q_ref,
):
    step = 8
    bins = 64
    far = far_ref[...]
    q_ref[...] = dot32(near_ref[...], wq_ref[...])
    base = dot32(far, wkv_ref[...])
    far_xyz = [jnp.broadcast_to(far[:, 64 + c : 65 + c], (COLS, LANES)) for c in range(3)]
    lane = iota((1, LANES), 1)
    centers = (lane % bins).astype(F32) * (RADIAL_REACH / (bins - 1))
    width = bins / RADIAL_REACH
    of_lane, to_lane = iota((LANES, LANES), 0), iota((LANES, LANES), 1)
    head_sum = jnp.where((of_lane < 64) & (of_lane // 16 == (to_lane % 64) // 16), 1.0, 0.0)
    ones = jnp.ones((64, LANES), BF16)
    cell = iota((COLS, 64), 0) + start_ref[0]
    slot = lane % 16

    def some(block, carry):
        first = pl.multiple_of(block * step, step)
        offsets, bases, counts, queries = [], [], [], []
        neigh = neigh_ref[pl.ds(first, step), :]
        q_some = q_ref[pl.ds(first, step), :]
        for u in range(step):
            off = [far_xyz[c] - xyz_ref[c, first + u] for c in range(3)]
            spacing = jnp.sqrt(off[0] * off[0] + off[1] * off[1] + off[2] * off[2] + 1e-06)
            away = (spacing - centers) * width
            bases.append(jnp.exp(-(away * away)))
            offsets.append(off)
            counts.append(jnp.where(cell == neigh[u : u + 1, :], 1.0, 0.0).astype(BF16))
            queries.append(q_some[u : u + 1, :])
        cells = pair_ref[pl.ds(first, step)].reshape(step * COLS, CH)
        edge = dot(cells, ep_ref[...]) + dot32(jnp.concatenate(bases, 0), er_ref[...])
        count = dot(jnp.concatenate(counts, 0), ones)
        edges, products = [], []
        for u in range(step):
            one = edge[u * COLS : (u + 1) * COLS] + base
            edges.append(one)
            products.append(one * queries[u])
        scores = dot32(jnp.concatenate(products, 0), head_sum)
        lines = []
        for u in range(step):
            times = count[u * COLS : (u + 1) * COLS]
            score = jnp.where(times > 0.0, scores[u * COLS : (u + 1) * COLS], NEGATIVE)
            top = jnp.max(score, axis=0, keepdims=True)
            w = times * jnp.exp(score - top)
            total = jnp.sum(w, axis=0, keepdims=True)
            shift = [jnp.sum(w * offsets[u][c], axis=0, keepdims=True) for c in range(3)]
            value = jnp.sum(w * edges[u], axis=0, keepdims=True)
            small = jnp.where(slot == 0, top, 0.0)
            for at, entry in enumerate([total] + shift):
                small = jnp.where(slot == at + 1, entry, small)
            lines.append(jnp.where(lane < 64, small, value))
        out_ref[pl.ds(first, step), :] = jnp.concatenate(lines, 0)
        return carry

    lax.fori_loop(0, ROWS // step, some, 0)


def merge_kernel(gain_ref, parts_ref, near_ref, wo_ref, out_ref):
    of_lane, to_lane = iota((LANES, LANES), 0), iota((LANES, LANES), 1)
    home = ((to_lane % 64) // 16) * 16
    to_top = jnp.where(of_lane == home, 1.0, 0.0)
    to_total = jnp.where(of_lane == home + 1, 1.0, 0.0)
    gain = jnp.zeros((LANES, LANES), F32)
    for head in range(4):
        for c in range(3):
            at = (of_lane == head * 16 + 2 + c) & (to_lane == 64 + c)
            gain = jnp.where(at, gain_ref[head], gain)
    count = parts_ref.shape[0]
    parts = [parts_ref[p] for p in range(count)]
    tops = [dot32(part, to_top) for part in parts]
    highest = functools.reduce(jnp.maximum, tops)
    merged = sum(jnp.exp(top - highest) * part for top, part in zip(tops, parts))
    ratio = merged / dot32(merged, to_total)
    out_ref[...] = near_ref[...] + dot32(ratio, wo_ref[...] + gain)


def widen(weight_ref, wide_ref, column):
    weight = weight_ref[...].astype(F32)
    lane = iota((CH, LANES), 1)
    for h in range(HEADS):
        for i in range(4):
            turned = pltpu.roll(weight, ((i - h) * SLOT) % LANES, 1) if i != h else weight
            wide_ref[i * CH : (i + 1) * CH, column + h * LANES : column + (h + 1) * LANES] = (
                jnp.where(lane // SLOT == i, turned, 0.0).astype(BF16)
            )


def widen_out(weight_ref, wide_ref):
    wide_ref[...] = jnp.zeros_like(wide_ref)
    for h in range(HEADS):
        for i in range(4):
            wide_ref[
                h * LANES + i * SLOT : h * LANES + (i + 1) * SLOT, i * CH : (i + 1) * CH
            ] = weight_ref[h * SLOT : (h + 1) * SLOT, :]


def normed(rounded, norm_gain):
    mean_of = jnp.full((CH, LANES), 1.0 / CH, BF16)
    centered = rounded.astype(F32) - dot(rounded, mean_of)
    high, low = split(centered * centered)
    spread = dot(high, mean_of) + dot(low, mean_of)
    return centered * lax.rsqrt(spread + 1e-05) * norm_gain


def spread_mask(mask, group):
    n = mask.shape[1]
    pick = iota((n, LANES), 0) == 4 * group + iota((n, LANES), 1) // SLOT
    return dot(mask, jnp.where(pick, 1.0, 0.0).astype(BF16))


def put_projections(z, mask, wide_ref, put):
    scales = (1.0 / math.sqrt(SLOT), 1.0 / math.sqrt(LENGTH))
    for matrix in range(4):
        wide = HEADS * LANES
        out = dot(z, wide_ref[:, matrix * wide : (matrix + 1) * wide])
        for h in range(HEADS):
            one = out[:, h * LANES : (h + 1) * LANES]
            if matrix < 2:
                one = one * mask * scales[matrix]
            put(matrix, h, one)


def row_start_kernel(
    xyz_ref, pair_ref, far_ref, mask_ref, radial_ref, gain_ref, wq_ref, wk_ref, wv_ref, wg_ref,
    x_ref, qkv_ref, gate_ref, z_ref, wide_ref,
):
    bins = 64
    for at, ref in enumerate((wq_ref, wk_ref, wv_ref, wg_ref)):
        widen(ref, wide_ref, at * HEADS * LANES)
    far = far_ref[...]
    far_xyz = [jnp.broadcast_to(far[:, 64 + c : 65 + c], (COLS, LANES)) for c in range(3)]
    lane = iota((1, LANES), 1)
    centers = (lane % bins).astype(F32) * (RADIAL_REACH / (bins - 1))
    width = bins / RADIAL_REACH
    table = radial_ref[...]
    blank = jnp.zeros_like(table)
    table = jnp.concatenate(
        [jnp.concatenate([table, blank], 1), jnp.concatenate([blank, table], 1)], 0
    )
    table_high, table_low = split(table)
    table = jnp.concatenate([table_high, table_low, table_high], 0)
    norm_gain = gain_ref[...]

    def some(group, carry):
        bases = []
        for at in range(2):
            n = group * 4 + at * 2
            off = [
                far_xyz[c] - jnp.where(lane < bins, xyz_ref[c, n], xyz_ref[c, n + 1])
                for c in range(3)
            ]
            spacing = jnp.sqrt(off[0] * off[0] + off[1] * off[1] + off[2] * off[2] + 1e-06)
            away = (spacing - centers) * width
            bases.append(jnp.exp(-(away * away)))
        high, low = split(jnp.concatenate(bases, 0))
        added = dot(jnp.concatenate([high, high, low], 1), table)
        rows = []
        for i in range(4):
            at = (i // 2) * COLS
            part = added[at : at + COLS, (i % 2) * CH : (i % 2 + 1) * CH]
            rows.append((pair_ref[group * 4 + i].astype(F32) + part).astype(BF16))
            x_ref[group * 4 + i] = rows[-1]
        z = normed(jnp.concatenate(rows, 0), norm_gain).astype(BF16)
        for i in range(4):
            z_ref[pl.ds(pl.multiple_of(group * COLS, COLS), COLS), i * CH : (i + 1) * CH] = z[
                i * COLS : (i + 1) * COLS
            ]
        return carry

    groups = ROWS // 4
    lax.fori_loop(0, groups, some, 0)
    size = groups // 2 * COLS
    for s in range(2):
        mask = jnp.concatenate(
            [spread_mask(mask_ref[...], s * (groups // 2) + g) for g in range(groups // 2)], 0
        )

        def put(matrix, h, one):
            if matrix < 3:
                qkv_ref[h * 2 + s, matrix] = one.astype(BF16)
            else:
                gate_ref[h, s] = jax.nn.sigmoid(one)

        put_projections(z_ref[s * size : (s + 1) * size, :], mask, wide_ref, put)


def gathered(parts_ref, which, g, across):
    count = parts_ref.shape[0]
    if across == COLS:
        return jnp.concatenate(
            [parts_ref[p, which, g * across : (g + 1) * across, :] for p in range(count)], 0
        )
    return jnp.concatenate(
        [
            parts_ref[p, which].astype(F32)[g * across : (g + 1) * across]
            for p in range(count)
        ],
        0,
    ).astype(BF16)


def logits_kernel(across, core_ref, qkv_ref, own_ref, other_ref, q_ref, k_ref, sum_ref):
    for g in range(5):
        q_ref[:, g * LANES : (g + 1) * LANES] = gathered(qkv_ref, 0, g, across)
        k_ref[:, g * LANES : (g + 1) * LANES] = gathered(qkv_ref, 1, g, across)
    rows = 128
    for m in range(LENGTH // rows):
        sum_ref[m * rows : (m + 1) * rows, :] = lax.dot_general(
            q_ref[m * rows : (m + 1) * rows, :],
            k_ref[...],
            (((1,), (1,)), ((), ())),
            preferred_element_type=F32,
        )
    core = core_ref[0]
    own_ref[...] = sum_ref[pl.ds(pl.multiple_of(core * HALF, HALF), HALF), :]
    other_ref[...] = sum_ref[pl.ds(pl.multiple_of((1 - core) * HALF, HALF), HALF), :].astype(BF16)


def join_kernel(own_ref, other_ref, out_ref):
    out_ref[OWNERS:] = jnp.zeros((out_ref.shape[0] - OWNERS, BLOCK, LENGTH), BF16)
    for m in range(OWNERS):
        at = slice(m * BLOCK, (m + 1) * BLOCK)
        out_ref[m] = (own_ref[at, :] + other_ref[at, :].astype(F32)).astype(BF16)


def bias_kernel(weight_ref, near_ref, far_ref, out_ref):
    bins = 64
    near, far = near_ref[...], far_ref[...]
    square = jnp.zeros((BLOCK, LENGTH), F32)
    for c in range(3):
        off = near[:, c : c + 1] - far[c : c + 1, :]
        square = square + off * off
    width = bins / RADIAL_REACH
    spacing = jnp.sqrt(square + 1e-06) * width

    def some(at, total):
        for u in range(8):
            b = at * 8 + u
            away = spacing - b.astype(F32) * (width * RADIAL_REACH / (bins - 1))
            total = total + weight_ref[b] * jnp.exp(-(away * away))
        return total

    out_ref[...] = lax.fori_loop(0, bins // 8, some, jnp.zeros((BLOCK, LENGTH), F32))


def softmax_kernel(parts_ref, bias_ref, out_ref):
    count = parts_ref.shape[0]
    logits = bias_ref[...]
    for p in range(count):
        logits = logits + parts_ref[p].astype(F32)
    scaled = jnp.exp(logits - jnp.max(logits, axis=-1, keepdims=True))
    weights = (scaled / jnp.sum(scaled, axis=-1, keepdims=True)).astype(BF16)
    for p in range(count):
        out_ref[p] = weights


def mix_kernel(across, core_ref, own_ref, other_ref, qkv_ref, out_ref, a_ref, v_ref):
    core = core_ref[0]
    for m in range(OWNERS):
        at = pl.multiple_of(core * HALF + m * BLOCK, BLOCK)
        a_ref[pl.ds(at, BLOCK), :] = own_ref[m]
        at = pl.multiple_of((1 - core) * HALF + m * BLOCK, BLOCK)
        a_ref[pl.ds(at, BLOCK), :] = other_ref[m]
    for g in range(5):
        v_ref[:, g * LANES : (g + 1) * LANES] = gathered(qkv_ref, 2, g, across)
    rows = 160
    for m in range(LENGTH // rows):
        mixed = dot(a_ref[m * rows : (m + 1) * rows, :], v_ref[...])
        for p in range(rows // across):
            pieces = [
                mixed[p * across : (p + 1) * across, g * LANES : (g + 1) * LANES]
                for g in range(5)
            ]
            spare = out_ref.shape[1] - 5 * across
            if spare:
                pieces.append(jnp.zeros((spare, LANES), F32))
            out_ref[m * (rows // across) + p] = jnp.concatenate(pieces, 0).astype(BF16)


def column_start_kernel(
    x_ref, gate_ref, mixed_ref, mask_ref, wo_ref, gain_ref, wq_ref, wk_ref, wv_ref, wg_ref,
    new_ref, qkv_ref, next_gate_ref, z_ref, wide_out_ref, wide_ref,
):
    widen_out(wo_ref, wide_out_ref)
    for at, ref in enumerate((wq_ref, wk_ref, wv_ref, wg_ref)):
        widen(ref, wide_ref, at * HEADS * LANES)
    norm_gain = gain_ref[...]
    for s in range(2):
        gated = jnp.concatenate(
            [
                (gate_ref[h, s] * mixed_ref[h * 2 + s].astype(F32)).astype(BF16)
                for h in range(HEADS)
            ],
            1,
        )
        update = dot(gated, wide_out_ref[...])
        for g in range(5):
            rows = []
            for i in range(4):
                n = (s * 5 + g) * 4 + i
                part = update[g * COLS : (g + 1) * COLS, i * CH : (i + 1) * CH]
                rows.append((x_ref[n].astype(F32) + part).astype(BF16))
                new_ref[n] = rows[-1]
            z = normed(jnp.concatenate(rows, 0), norm_gain)
            first = (s * 5 + g) * 4 * COLS
            z_ref[first : first + 4 * COLS, :] = z
    for chunk in range(4):
        pieces, masks = [], []
        for g in range(5):
            column = (chunk * 5 + g) * 4
            pieces.append(
                jnp.concatenate(
                    [z_ref[pl.ds(column + i, ROWS, stride=COLS), :] for i in range(4)], 1
                )
            )
            masks.append(spread_mask(mask_ref[...], chunk * 5 + g))

        def put(matrix, h, one):
            if matrix < 3:
                spare = qkv_ref.shape[2] - one.shape[0]
                qkv_ref[h * 4 + chunk, matrix] = jnp.concatenate(
                    [one, jnp.zeros((spare, LANES), F32)], 0
                ).astype(BF16)
            else:
                next_gate_ref[h, chunk] = jax.nn.sigmoid(one)

        put_projections(
            jnp.concatenate(pieces, 0).astype(BF16), jnp.concatenate(masks, 0), wide_ref, put
        )


def finish_kernel(x_ref, gate_ref, mixed_ref, wo_ref, out_ref, turned_ref, wide_out_ref):
    widen_out(wo_ref, wide_out_ref)
    for chunk in range(4):
        gated = jnp.concatenate(
            [
                gate_ref[h, chunk] * mixed_ref[h * 4 + chunk].astype(F32)[: 5 * ROWS]
                for h in range(HEADS)
            ],
            1,
        ).astype(BF16)
        update = dot(gated, wide_out_ref[...])
        for g in range(5):
            for i in range(4):
                column = (chunk * 5 + g) * 4 + i
                turned_ref[pl.ds(column, ROWS, stride=COLS), :] = update[
                    g * ROWS : (g + 1) * ROWS, i * CH : (i + 1) * CH
                ]
    for n in range(ROWS):
        out_ref[n] = (x_ref[n].astype(F32) + turned_ref[n * COLS : (n + 1) * COLS, :]).astype(BF16)


def exchange(parts, axes):
    return lax.all_to_all(parts, axes, split_axis=0, concat_axis=0, tiled=True)


def swap_cores(x):
    return lax.ppermute(x, "core", [(0, 1), (1, 0)])


def column_tokens(mine, row, cols_n):
    device = lambda r, c: r * cols_n + c
    half = cols_n
    rows_n = 2 * cols_n
    ways = []
    for flip in (0, 1):
        pairs = [
            (device(r, c), device(c + half * ((r % 2) ^ flip), r // 2))
            for r in range(rows_n)
            for c in range(cols_n)
        ]
        ways.append(lax.ppermute(mine, EVERYWHERE, pairs))
    lower = row < half
    return jnp.concatenate(
        [jnp.where(lower, ways[0], ways[1]), jnp.where(lower, ways[1], ways[0])], 0
    )


def tied_attention(across, qkv, core, bias, sum_axes, pass_axes):
    own, other = call(
        functools.partial(logits_kernel, across),
        (shape((HALF, LENGTH), F32), shape((HALF, LENGTH), BF16)),
        [SMEM, VMEM],
        [
            pltpu.VMEM((LENGTH, 5 * LANES), BF16),
            pltpu.VMEM((LENGTH, 5 * LANES), BF16),
            pltpu.VMEM((LENGTH, LENGTH), F32),
        ],
    )(core, qkv)
    parts = call(join_kernel, shape((16, BLOCK, LENGTH), BF16), [VMEM] * 2)(own, swap_cores(other))
    weights = call(softmax_kernel, shape((16, BLOCK, LENGTH), BF16), [VMEM] * 2)(
        exchange(parts, sum_axes), bias
    )
    own = exchange(weights, sum_axes)[:OWNERS]
    other = swap_cores(own)
    mixed = call(
        functools.partial(mix_kernel, across),
        shape((qkv.shape[0],) + qkv.shape[2:], BF16),
        [SMEM, VMEM, VMEM, VMEM],
        [pltpu.VMEM((LENGTH, LENGTH), BF16), pltpu.VMEM((LENGTH, 5 * LANES), BF16)],
    )(core, own, other, qkv)
    return exchange(mixed, pass_axes)


def shards(
    pair, pair_mask, node_state, coords, neighbours, atom_type, type_table, node_query, node_key,
    node_value, edge_pair, edge_radial, node_out_w, coord_gain, radial_pair, row_gain, row_query,
    row_key, row_value, row_gate, row_out, row_bias, column_gain, column_query, column_key,
    column_value, column_gate, column_out, column_bias,
):
    rows_n, cols_n, channels = pair.shape
    row, col = lax.axis_index(("x", "y")), lax.axis_index(("z", "core"))
    core = lax.axis_index("core")[None].astype(jnp.int32)
    node_width = node_state.shape[1]
    onehot = (atom_type[:, None] == jnp.arange(type_table.shape[0], dtype=jnp.int32)[None, :])
    features = node_state + jnp.dot(onehot.astype(F32), type_table, precision=PRECISE)
    spare = LANES - node_width
    near = jnp.concatenate(
        [features, coords.T, jnp.zeros((rows_n, spare - coords.shape[0]), F32)], 1
    )
    far = column_tokens(near, row, 8)
    wq = jnp.pad(node_query * 0.25, ((0, spare), (0, spare)))
    wkv = jnp.pad(jnp.concatenate([node_key, node_value], 1), ((0, spare), (0, 0)))
    er = jnp.pad(edge_radial, ((0, LANES - edge_radial.shape[0]), (0, 0)))
    wo = jnp.pad(node_out_w, ((spare, 0), (0, spare)))
    start = (col * cols_n)[None].astype(jnp.int32)
    part = call(
        graph_kernel,
        shape((ROWS, LANES), F32),
        [SMEM, SMEM] + [VMEM] * 8,
        [pltpu.VMEM((ROWS, LANES), F32)],
    )(start, coords, pair, near, far, neighbours, wq, wkv, edge_pair, er)
    parts = exchange(jnp.broadcast_to(part[None], (8,) + part.shape), ("z", "core"))
    updated = call(merge_kernel, shape((ROWS, LANES), F32), [SMEM] + [VMEM] * 3)(
        coord_gain, parts, near, wo
    )
    new_state = updated[:, :node_width]
    new_coords = updated[:, node_width : node_width + 3].T
    far = column_tokens(updated, row, 8)
    all_xyz = lax.all_gather(new_coords, ("x", "y"), axis=1, tiled=True)

    groups = ROWS // 4
    projected = lambda count, size: [
        shape((ROWS, COLS, CH), BF16),
        shape((count, 3, size, LANES), BF16),
    ]
    x, qkv, gate = call(
        row_start_kernel,
        (*projected(8, 400), shape((HEADS, 2, 400, LANES), F32)),
        [SMEM] + [VMEM] * 9,
        [
            pltpu.VMEM((groups * COLS, 4 * CH), BF16),
            pltpu.VMEM((4 * CH, 4 * HEADS * LANES), BF16),
        ],
    )(
        new_coords, pair, far, pair_mask.T.astype(BF16), radial_pair, row_gain[None],
        row_query, row_key, row_value, row_gate,
    )

    def bias(weight, head, place):
        first = core[0] * HALF + jnp.minimum(place, OWNERS - 1) * BLOCK
        tokens = lax.dynamic_slice_in_dim(all_xyz, first, BLOCK, 1).T
        return call(bias_kernel, shape((BLOCK, LENGTH), F32), [SMEM, VMEM, VMEM])(
            lax.dynamic_index_in_dim(weight, head, 1, keepdims=False), tokens, all_xyz
        )

    row_biases = bias(row_bias, lax.axis_index("z"), row)
    column_biases = bias(column_bias, lax.axis_index("x"), lax.axis_index(("y", "z")))
    mixed = tied_attention(
        COLS, exchange(qkv, ("z", "core")), core, row_biases, ("x", "y"), ("z", "core")
    )
    x, qkv, gate = call(
        column_start_kernel,
        (*projected(16, 208), shape((HEADS, 4, 200, LANES), F32)),
        [VMEM] * 10,
        [
            pltpu.VMEM((ROWS * COLS, CH), F32),
            pltpu.VMEM((HEADS * LANES, 4 * CH), BF16),
            pltpu.VMEM((4 * CH, 4 * HEADS * LANES), BF16),
        ],
    )(
        x, gate, mixed.reshape(8, 400, LANES), pair_mask.astype(BF16), row_out,
        column_gain[None], column_query, column_key, column_value, column_gate,
    )
    mixed = tied_attention(
        ROWS, exchange(qkv, ("x", "y")), core, column_biases, ("y", "z"), ("x", "y")
    )
    pair_out = call(
        finish_kernel,
        shape((ROWS, COLS, CH), BF16),
        [VMEM] * 4,
        [
            pltpu.VMEM((ROWS * COLS, CH), F32),
            pltpu.VMEM((HEADS * LANES, 4 * CH), BF16),
        ],
    )(x, gate, mixed, column_out)
    return (pair_out, new_state, new_coords)


def solution(mesh):
    cube = Mesh(mesh.devices.reshape(4, 4, 4, 2), EVERYWHERE)
    row, col = ("x", "y"), ("z", "core")
    placed = (
        P(row, col, None), P(row, col), P(row, None), P(None, row), P(row, None), P(row),
    ) + (P(),) * 23
    return jax.shard_map(
        shards,
        mesh=cube,
        in_specs=placed,
        out_specs=(P(row, col, None), P(row, None), P(None, row)),
        check_vma=False,
    )
```

```python
import functools
import math

import jax
import jax.numpy as jnp
from jax import lax
from jax.experimental import pallas as pl
from jax.experimental.pallas import tpu as pltpu
from jax.sharding import Mesh
from jax.sharding import PartitionSpec as P

BF16 = jnp.bfloat16
F32 = jnp.float32
PRECISE = lax.Precision.HIGHEST
RADIAL_REACH = 24.0
NEGATIVE = -1e30
EVERYWHERE = ("x", "y", "z", "core")

VMEM = pl.BlockSpec(memory_space=pltpu.VMEM)
SMEM = pl.BlockSpec(memory_space=pltpu.SMEM)
MIB = 1024 * 1024

ROWS, COLS, CH, HEADS = 40, 80, 128, 4
LENGTH = 640
LANES = 128
SLOT = 32
BLOCK = 24
OWNERS = 14
HALF = LENGTH // 2


def call(kernel, out_shape, in_specs, scratch=(), limit=44):
    out_specs = jax.tree.map(lambda _: VMEM, out_shape)
    return pl.pallas_call(
        kernel,
        out_shape=out_shape,
        in_specs=in_specs,
        out_specs=out_specs,
        scratch_shapes=list(scratch),
        compiler_params=pltpu.CompilerParams(vmem_limit_bytes=limit * MIB),
    )


def shape(dims, dtype):
    return jax.ShapeDtypeStruct(dims, dtype)


def iota(dims, axis):
    return lax.broadcasted_iota(jnp.int32, dims, axis)


def dot(a, b):
    return jnp.dot(a, b, preferred_element_type=F32)


def dot32(a, b):
    return jnp.dot(a, b, preferred_element_type=F32, precision=PRECISE)


def length_of(square):
    square = square + 1e-06
    return square * lax.rsqrt(square)


def split(a):
    high = a.astype(BF16)
    return high, (a - high.astype(F32)).astype(BF16)


def split3(a):
    high, low = split(a)
    return high, low, (a - high.astype(F32) - low.astype(F32)).astype(BF16)


def graph_kernel(
    place_ref, xyz_ref, near_ref, way0_ref, way1_ref, pair_ref, neigh_ref, wq_ref, wk_ref, wv_ref,
    ep_ref, er_ref, small_ref, values_ref, q_ref, sums_ref,
):
    step = 8
    bins = 64
    lower = place_ref[1] == 1
    way0, way1 = way0_ref[...], way1_ref[...]
    far = jnp.concatenate([jnp.where(lower, way0, way1), jnp.where(lower, way1, way0)], 0)
    blank = jnp.zeros((64, LANES), F32)
    wq = jnp.concatenate([wq_ref[...] * 0.25, jnp.zeros((64, 64), F32)], 1)
    q_ref[...] = dot32(near_ref[...], jnp.concatenate([wq, blank], 0))
    wkv = jnp.concatenate([wk_ref[...], wv_ref[...]], 1)
    base = dot32(far, jnp.concatenate([wkv, blank], 0))
    far_xyz = [jnp.broadcast_to(far[:, 64 + c : 65 + c], (COLS, LANES)) for c in range(3)]
    lane = iota((1, LANES), 1)
    centers = (lane % bins).astype(F32) * (RADIAL_REACH / (bins - 1))
    width = bins / RADIAL_REACH
    of_lane, to_lane = iota((LANES, LANES), 0), iota((LANES, LANES), 1)
    to_value = (of_lane < 64) & (of_lane // 16 == (to_lane % 64) // 16)
    to_small = (of_lane < 64) & (of_lane // 16 == jnp.minimum(to_lane % 24 // 5, 3))
    head_sum = jnp.concatenate(
        [jnp.where(to_value, 1.0, 0.0), jnp.where(to_small, 1.0, 0.0)], 1
    ).astype(BF16)
    head_sum = jnp.concatenate([head_sum] * 3, 0)
    table_high, table_low = split(er_ref[...])
    table = jnp.concatenate([table_high, table_high, table_low, jnp.zeros_like(table_low)], 0)
    ones = jnp.ones((64, LANES), BF16)
    cell = iota((COLS, 64), 0) + place_ref[0]
    place = lane % 24
    slot = jnp.where(place < 20, place % 5, place - 15)

    def some(block, small):
        first = pl.multiple_of(block * step, step)
        offsets, bases, counts, queries = [], [], [], []
        neigh = neigh_ref[pl.ds(first, step), :]
        q_some = q_ref[pl.ds(first, step), :]
        for u in range(step):
            off = [far_xyz[c] - xyz_ref[c, first + u] for c in range(3)]
            spacing = length_of(off[0] * off[0] + off[1] * off[1] + off[2] * off[2])
            away = (spacing - centers) * width
            bases.append(jnp.exp(-(away * away)))
            offsets.append(off)
            counts.append(jnp.where(cell == neigh[u : u + 1, :], 1.0, 0.0).astype(BF16))
            queries.append(q_some[u : u + 1, :])
        cells = pair_ref[pl.ds(first, step)].reshape(step * COLS, CH)
        high, low = split(jnp.concatenate(bases, 0))
        bases = jnp.concatenate([jnp.where(lane < bins, high, low), high], 1)
        edge = dot(cells, ep_ref[...]) + dot(bases, table)
        count = dot(jnp.concatenate(counts, 0), ones)
        edges, products = [], []
        for u in range(step):
            one = edge[u * COLS : (u + 1) * COLS] + base
            edges.append(one)
            products.append(one * queries[u])
        scores = dot(jnp.concatenate(split3(jnp.concatenate(products, 0)), 1), head_sum)
        lines, sums = [], []
        for u in range(step):
            times = count[u * COLS : (u + 1) * COLS]
            score = scores[u * COLS : (u + 1) * COLS]
            both = []
            for part in (score[:, :LANES], score[:, LANES:]):
                part = jnp.where(times > 0.0, part, NEGATIVE)
                top = jnp.max(part, axis=0, keepdims=True)
                both.append((top, times * jnp.exp(part - top)))
            (_, for_value), (top, w) = both
            sums.append(jnp.sum(for_value * edges[u], axis=0, keepdims=True))
            entries = [top, jnp.sum(w, axis=0, keepdims=True)]
            entries += [jnp.sum(w * offsets[u][c], axis=0, keepdims=True) for c in range(3)]
            entries += [xyz_ref[c, first + u] for c in range(3)]
            line = jnp.zeros((1, LANES), F32)
            for at, entry in enumerate(entries):
                line = jnp.where(slot == at, entry, line)
            lines.append(line)
        sums_ref[pl.ds(first, step), :] = jnp.concatenate(sums, 0)
        return jnp.where(lane // 24 == block, jnp.concatenate(lines, 0), small)

    small = lax.fori_loop(0, ROWS // step, some, jnp.zeros((step, LANES), F32))
    small_ref[...] = jnp.broadcast_to(small[None], small_ref.shape)
    sums = sums_ref[...]
    turned = pltpu.roll(sums, 64, 1)
    high = turned.astype(BF16).astype(F32)
    low = sums - sums.astype(BF16).astype(F32)
    values = jnp.where(lane < 64, high, low)
    values_ref[...] = jnp.concatenate([values, jnp.zeros((8, LANES), F32)], 0).astype(BF16)


def merge_kernel(gain_ref, parts_ref, out_ref):
    of_lane, to_lane = iota((LANES, LANES), 0), iota((LANES, LANES), 1)
    first = jnp.where(to_lane < 120, to_lane // 24 * 24, 0)
    home = first + jnp.minimum(to_lane % 24 // 5, 3) * 5
    to_top = jnp.where(of_lane == home, 1.0, 0.0).astype(BF16)
    to_total = jnp.where(of_lane == home + 1, 1.0, 0.0)
    start = to_lane // 3 * 24
    gain = jnp.zeros((LANES, LANES), F32)
    for head in range(4):
        at = (of_lane == start + head * 5 + 2 + to_lane % 3) & (to_lane < 15)
        gain = jnp.where(at, gain_ref[head], gain)
    to_old = jnp.where((of_lane == start + 20 + to_lane % 3) & (to_lane < 15), 1.0, 0.0)
    parts = parts_ref[...].reshape(128 * 8, LANES)
    tops = dot(jnp.concatenate(split3(parts), 1), jnp.concatenate([to_top] * 3, 0))
    merged, old = [], []
    for row in range(16):
        some = [slice((row * 8 + p) * 8, (row * 8 + p + 1) * 8) for p in range(8)]
        highest = functools.reduce(jnp.maximum, [tops[at] for at in some])
        merged.append(sum(jnp.exp(tops[at] - highest) * parts[at] for at in some))
        old.append(parts[some[0]])
    merged = jnp.concatenate(merged, 0)
    ratio = merged / dot32(merged, to_total)
    new = dot32(jnp.concatenate(old, 0), to_old) + dot32(ratio, gain)
    out_ref[...] = new.reshape(16, 8, LANES)


def node_kernel(place_ref, parts_ref, sent_ref, near_ref, wo_ref, out_ref):
    lane = iota((8, LANES), 1)
    of_lane, to_lane = iota((LANES, LANES), 0), iota((LANES, LANES), 1)
    parts = [parts_ref[place_ref[2] * 8 + p] for p in range(8)]
    values = [sent_ref[p, sent_ref.shape[1] - 48 :, :].astype(F32) for p in range(8)]
    values = [value + pltpu.roll(value, 64, 1) for value in values]
    stacked = jnp.concatenate(parts, 0)
    attended = []
    for g in range(5):
        home = g * 24 + (to_lane % 64) // 16 * 5 + to_lane // 64
        both = dot32(stacked, jnp.where(of_lane == home, 1.0, 0.0))
        tops = [both[p * 8 : (p + 1) * 8] for p in range(8)]
        highest = functools.reduce(jnp.maximum, tops)
        above, below = 0.0, 0.0
        for p in range(8):
            scale = jnp.exp(tops[p] - highest)
            above = above + scale * values[p][g * 8 : (g + 1) * 8]
            below = below + scale * pltpu.roll(tops[p], 64, 1)
        attended.append(jnp.where(lane < 64, above / jnp.where(lane < 64, below, 1.0), 0.0))
    attended = jnp.concatenate(attended, 0)[:, :64]
    out_ref[...] = near_ref[...][:, :64] + dot32(attended, wo_ref[...])


def widen(weight, wide_ref, column):
    weight = weight.astype(F32)
    lane = iota((CH, LANES), 1)
    for h in range(HEADS):
        for i in range(4):
            turned = pltpu.roll(weight, ((i - h) * SLOT) % LANES, 1) if i != h else weight
            wide_ref[i * CH : (i + 1) * CH, column + h * LANES : column + (h + 1) * LANES] = (
                jnp.where(lane // SLOT == i, turned, 0.0).astype(BF16)
            )


def widen_out(weight, wide_ref):
    wide_ref[...] = jnp.zeros_like(wide_ref)
    for h in range(HEADS):
        for i in range(4):
            wide_ref[
                h * LANES + i * SLOT : h * LANES + (i + 1) * SLOT, i * CH : (i + 1) * CH
            ] = weight[h * SLOT : (h + 1) * SLOT, :]


def normed(rounded, norm_gain):
    mean_of = jnp.full((CH, LANES), 1.0 / CH, BF16)
    centered = rounded.astype(F32) - dot(rounded, mean_of)
    high, low = split(centered * centered)
    spread = dot(jnp.concatenate([high, low], 1), jnp.concatenate([mean_of, mean_of], 0))
    return centered * lax.rsqrt(spread + 1e-05) * norm_gain


def spread_mask(mask, group):
    n = mask.shape[1]
    pick = iota((n, LANES), 0) == 4 * group + iota((n, LANES), 1) // SLOT
    return dot(mask, jnp.where(pick, 1.0, 0.0).astype(BF16))


def put_projections(z, mask, wide_ref, put):
    scales = (1.0 / math.sqrt(SLOT), 1.0 / math.sqrt(LENGTH))
    for matrix in range(3):
        wide = HEADS * LANES
        out = dot(z, wide_ref[:, matrix * wide : (matrix + 1) * wide])
        for h in range(HEADS):
            one = out[:, h * LANES : (h + 1) * LANES]
            if matrix < 2:
                one = one * mask * scales[matrix]
            put(matrix, h, one)


def gate_kernel(z_ref, weight_ref, gate_ref, wide_ref):
    widen(weight_ref[...], wide_ref, 0)
    for block in range(z_ref.shape[0]):
        out = jax.nn.sigmoid(dot(z_ref[block], wide_ref[...]))
        for h in range(HEADS):
            gate_ref[h, block] = out[:, h * LANES : (h + 1) * LANES].astype(BF16)


def row_start_kernel(
    place_ref, xyz_ref, new_ref, sums_ref, pair_ref, mask_ref, radial_ref, gain_ref, weights_ref,
    x_ref, qkv_ref, z_ref, wide_ref,
):
    bins = 64
    for at in range(3):
        widen(weights_ref[at * CH : (at + 1) * CH, :], wide_ref, at * HEADS * LANES)
    far = [new_ref[place_ref[0] * 2 + half] for half in range(2)]
    far_xyz = [
        jnp.concatenate(
            [
                jnp.broadcast_to(part[:, g * 3 + c : g * 3 + c + 1], (8, LANES))
                for part in far
                for g in range(5)
            ],
            0,
        )
        for c in range(3)
    ]
    row = place_ref[2]
    lane = iota((1, LANES), 1)
    centers = (lane % bins).astype(F32) * (RADIAL_REACH / (bins - 1))
    width = bins / RADIAL_REACH
    table = radial_ref[...]
    blank = jnp.zeros_like(table)
    table = jnp.concatenate(
        [jnp.concatenate([table, blank], 1), jnp.concatenate([blank, table], 1)], 0
    )
    table_high, table_low = split(table)
    table = jnp.concatenate([table_high, table_low, table_high], 0)
    norm_gain = gain_ref[...]

    together = 2
    size = ROWS // 8 * COLS

    def some(step, carry):
        bases, rows = [], []
        for at in range(2 * together):
            n = (step * together * 2 + at) * 2
            off = [
                far_xyz[c]
                - jnp.where(
                    lane < bins,
                    xyz_ref[row, n & 7, (n >> 3) * 3 + c],
                    xyz_ref[row, (n + 1) & 7, ((n + 1) >> 3) * 3 + c],
                )
                for c in range(3)
            ]
            spacing = length_of(off[0] * off[0] + off[1] * off[1] + off[2] * off[2])
            away = (spacing - centers) * width
            bases.append(jnp.exp(-(away * away)))
        high, low = split(jnp.concatenate(bases, 0))
        added = dot(jnp.concatenate([high, high, low], 1), table)
        for i in range(4 * together):
            at = (i // 2) * COLS
            n = step * together * 4 + i
            part = added[at : at + COLS, (i % 2) * CH : (i % 2 + 1) * CH]
            rows.append((pair_ref[n].astype(F32) + part).astype(BF16))
            x_ref[n] = rows[-1]
        z = normed(jnp.concatenate(rows, 0), norm_gain).astype(BF16)
        for i in range(4 * together):
            at = (step * together + i // 4) * COLS
            half, at = at // size, at % size
            z_ref[half, pl.ds(pl.multiple_of(at, COLS), COLS), (i % 4) * CH : (i % 4 + 1) * CH] = z[
                i * COLS : (i + 1) * COLS
            ]
        return carry

    groups = ROWS // 4
    lax.fori_loop(0, groups // together, some, 0)
    for s in range(2):
        for h in range(HEADS):
            qkv_ref[h * 2 + s, 3 * size :] = sums_ref[...]
        mask = jnp.concatenate(
            [spread_mask(mask_ref[...], s * (groups // 2) + g) for g in range(groups // 2)], 0
        )

        def put(matrix, h, one):
            qkv_ref[h * 2 + s, matrix * size : (matrix + 1) * size] = one.astype(BF16)

        put_projections(z_ref[s], mask, wide_ref, put)


def gathered(parts_ref, which, g, across):
    count = parts_ref.shape[0]
    if across == COLS:
        at = (which * 5 + g) * across
        return jnp.concatenate([parts_ref[p, at : at + across, :] for p in range(count)], 0)
    size = parts_ref.shape[1] // 3
    return jnp.concatenate(
        [
            parts_ref[p, which * size : (which + 1) * size].astype(F32)[
                g * across : (g + 1) * across
            ]
            for p in range(count)
        ],
        0,
    ).astype(BF16)


def logits_kernel(across, core_ref, qkv_ref, own_ref, other_ref, q_ref, k_ref, sum_ref):
    for g in range(5):
        q_ref[:, g * LANES : (g + 1) * LANES] = gathered(qkv_ref, 0, g, across)
        k_ref[:, g * LANES : (g + 1) * LANES] = gathered(qkv_ref, 1, g, across)
    rows = 128
    for m in range(LENGTH // rows):
        sum_ref[m * rows : (m + 1) * rows, :] = lax.dot_general(
            q_ref[m * rows : (m + 1) * rows, :],
            k_ref[...],
            (((1,), (1,)), ((), ())),
            preferred_element_type=F32,
        )
    core = core_ref[0]
    own_ref[...] = sum_ref[pl.ds(pl.multiple_of(core * HALF, HALF), HALF), :]
    other_ref[...] = sum_ref[pl.ds(pl.multiple_of((1 - core) * HALF, HALF), HALF), :].astype(BF16)


def join_kernel(own_ref, other_ref, out_ref):
    out_ref[OWNERS:] = jnp.zeros((out_ref.shape[0] - OWNERS, BLOCK, LENGTH), BF16)
    total = own_ref[...] + other_ref[...].astype(F32)
    spare = jnp.zeros((OWNERS * BLOCK - HALF, LENGTH), F32)
    total = jnp.concatenate([total, spare], 0)
    for m in range(OWNERS):
        out_ref[m] = total[m * BLOCK : (m + 1) * BLOCK].astype(BF16)


def bias_kernel(weight_ref, near_ref, far_ref, out_ref):
    bins = 64
    near, far = near_ref[...], far_ref[...]
    square = jnp.zeros((BLOCK, LENGTH), F32)
    for c in range(3):
        off = near[:, c : c + 1] - far[c : c + 1, :]
        square = square + off * off
    width = bins / RADIAL_REACH
    spacing = length_of(square) * width

    def some(at, total):
        for u in range(8):
            b = at * 8 + u
            away = spacing - b.astype(F32) * (width * RADIAL_REACH / (bins - 1))
            total = total + weight_ref[b] * jnp.exp(-(away * away))
        return total

    out_ref[...] = lax.fori_loop(0, bins // 8, some, jnp.zeros((BLOCK, LENGTH), F32))


def softmax_kernel(parts_ref, bias_ref, out_ref):
    count = parts_ref.shape[0]
    logits = bias_ref[...]
    for p in range(count):
        logits = logits + parts_ref[p].astype(F32)
    scaled = jnp.exp(logits - jnp.max(logits, axis=-1, keepdims=True))
    weights = (scaled / jnp.sum(scaled, axis=-1, keepdims=True)).astype(BF16)
    for p in range(count):
        out_ref[p] = weights


def mix_kernel(across, core_ref, own_ref, other_ref, parts_ref, out_ref, a_ref, v_ref):
    core = core_ref[0]
    for ref, half in ((own_ref, core), (other_ref, 1 - core)):
        rows = jnp.concatenate([ref[m].astype(F32) for m in range(OWNERS)], 0)[:HALF]
        a_ref[pl.ds(pl.multiple_of(half * HALF, HALF), HALF), :] = rows.astype(BF16)
    for g in range(5):
        v_ref[:, g * LANES : (g + 1) * LANES] = gathered(parts_ref, 2, g, across)
    rows = 160
    for m in range(LENGTH // rows):
        mixed = dot(a_ref[m * rows : (m + 1) * rows, :], v_ref[...])
        for p in range(rows // across):
            pieces = [
                mixed[p * across : (p + 1) * across, g * LANES : (g + 1) * LANES]
                for g in range(5)
            ]
            spare = out_ref.shape[1] - 5 * across
            if spare:
                pieces.append(jnp.zeros((spare, LANES), F32))
            out_ref[m * (rows // across) + p] = jnp.concatenate(pieces, 0).astype(BF16)


def column_start_kernel(
    x_ref, gate_ref, mixed_ref, mask_ref, gain_ref, weights_ref,
    new_ref, qkv_ref, turned_ref, z_ref, wide_out_ref, wide_ref,
):
    widen_out(weights_ref[3 * CH :, :], wide_out_ref)
    for at in range(3):
        widen(weights_ref[at * CH : (at + 1) * CH, :], wide_ref, at * HEADS * LANES)
    norm_gain = gain_ref[...]
    for s in range(2):
        gated = jnp.concatenate(
            [
                (gate_ref[h, s].astype(F32) * mixed_ref[h * 2 + s].astype(F32)).astype(BF16)
                for h in range(HEADS)
            ],
            1,
        )
        update = dot(gated, wide_out_ref[...])
        for g in range(5):
            rows = []
            for i in range(4):
                n = (s * 5 + g) * 4 + i
                part = update[g * COLS : (g + 1) * COLS, i * CH : (i + 1) * CH]
                rows.append((x_ref[n].astype(F32) + part).astype(BF16))
                new_ref[n] = rows[-1]
            z = normed(jnp.concatenate(rows, 0), norm_gain)
            first = (s * 5 + g) * 4 * COLS
            z_ref[first : first + 4 * COLS, :] = z
    for chunk in range(4):
        pieces, masks = [], []
        for g in range(5):
            column = (chunk * 5 + g) * 4
            pieces.append(
                jnp.concatenate(
                    [z_ref[pl.ds(column + i, ROWS, stride=COLS), :] for i in range(4)], 1
                )
            )
            masks.append(spread_mask(mask_ref[...], chunk * 5 + g))

        size = qkv_ref.shape[1] // 3
        z = jnp.concatenate(pieces, 0)
        spare = size - z.shape[0]
        z = jnp.concatenate([z, jnp.zeros((spare, z.shape[1]), F32)], 0).astype(BF16)
        turned_ref[chunk] = z
        mask = jnp.concatenate(masks + [jnp.zeros((spare, LANES), F32)], 0)

        def put(matrix, h, one):
            qkv_ref[h * 4 + chunk, matrix * size : (matrix + 1) * size] = one.astype(BF16)

        put_projections(z, mask, wide_ref, put)


def finish_kernel(x_ref, gate_ref, mixed_ref, wo_ref, out_ref, turned_ref, wide_out_ref):
    widen_out(wo_ref[...], wide_out_ref)
    for chunk in range(4):
        gated = jnp.concatenate(
            [
                gate_ref[h, chunk].astype(F32) * mixed_ref[h * 4 + chunk].astype(F32)
                for h in range(HEADS)
            ],
            1,
        ).astype(BF16)
        update = dot(gated, wide_out_ref[...])
        for g in range(5):
            for i in range(4):
                column = (chunk * 5 + g) * 4 + i
                turned_ref[pl.ds(column, ROWS, stride=COLS), :] = update[
                    g * ROWS : (g + 1) * ROWS, i * CH : (i + 1) * CH
                ]
    for n in range(ROWS):
        out_ref[n] = (x_ref[n].astype(F32) + turned_ref[n * COLS : (n + 1) * COLS, :]).astype(BF16)


def exchange(parts, axes):
    return lax.all_to_all(parts, axes, split_axis=0, concat_axis=0, tiled=True)


def swap_cores(x):
    return lax.ppermute(x, "core", [(0, 1), (1, 0)])


def column_tokens(mine, cols_n):
    device = lambda r, c: r * cols_n + c
    half = cols_n
    rows_n = 2 * cols_n
    ways = []
    for flip in (0, 1):
        pairs = [
            (device(r, c), device(c + half * ((r % 2) ^ flip), r // 2))
            for r in range(rows_n)
            for c in range(cols_n)
        ]
        ways.append(lax.ppermute(mine, EVERYWHERE, pairs))
    return ways


def tied_attention(across, qkv, core, bias, sum_axes, pass_axes, beside):
    own, other = call(
        functools.partial(logits_kernel, across),
        (shape((HALF, LENGTH), F32), shape((HALF, LENGTH), BF16)),
        [SMEM, VMEM],
        [
            pltpu.VMEM((LENGTH, 5 * LANES), BF16),
            pltpu.VMEM((LENGTH, 5 * LANES), BF16),
            pltpu.VMEM((LENGTH, LENGTH), F32),
        ],
    )(core, qkv)
    parts = call(join_kernel, shape((16, BLOCK, LENGTH), BF16), [VMEM] * 2)(own, swap_cores(other))
    parts = exchange(parts, sum_axes)
    weights = call(softmax_kernel, shape((16, BLOCK, LENGTH), BF16), [VMEM] * 2)(
        parts, bias
    )
    own, first = lax.optimization_barrier((exchange(weights, sum_axes)[:OWNERS], beside[0]))
    other = swap_cores(own)
    mixed = call(
        functools.partial(mix_kernel, across),
        shape((qkv.shape[0], 5 * across + 5 * across % 16, LANES), BF16),
        [SMEM, VMEM, VMEM, VMEM],
        [pltpu.VMEM((LENGTH, LENGTH), BF16), pltpu.VMEM((LENGTH, 5 * LANES), BF16)],
    )(core, own, other, qkv)
    mixed, second = lax.optimization_barrier((exchange(mixed, pass_axes), beside[1]))
    return mixed, first, second


def shards(
    pair, pair_mask, node_state, coords, neighbours, atom_type, type_table, node_query, node_key,
    node_value, edge_pair, edge_radial, node_out_w, coord_gain, radial_pair, row_gain, row_query,
    row_key, row_value, row_gate, row_out, row_bias, column_gain, column_query, column_key,
    column_value, column_gate, column_out, column_bias,
):
    rows_n, cols_n, channels = pair.shape
    row, col = lax.axis_index(("x", "y")), lax.axis_index(("z", "core"))
    core = lax.axis_index("core")[None].astype(jnp.int32)
    node_width = node_state.shape[1]
    onehot = (atom_type[:, None] == jnp.arange(type_table.shape[0], dtype=jnp.int32)[None, :])
    features = node_state + jnp.dot(onehot.astype(F32), type_table, precision=PRECISE)
    spare = LANES - node_width
    near = jnp.concatenate(
        [features, coords.T, jnp.zeros((rows_n, spare - coords.shape[0]), F32)], 1
    )
    ways = column_tokens(near, 8)
    place = jnp.stack([col * cols_n, (row < 8).astype(jnp.int32)]).astype(jnp.int32)
    remote = (pair, neighbours, node_query, node_key, node_value, edge_pair, edge_radial)
    small, sums = call(
        graph_kernel,
        (shape((128, 8, LANES), F32), shape((48, LANES), BF16)),
        [SMEM] * 2 + [VMEM] * 10,
        [pltpu.VMEM((ROWS, LANES), F32)] * 2,
        limit=60,
    )(place, coords, near, *ways, *remote)
    small, *weights = lax.optimization_barrier((small, row_query, row_key, row_value))
    weights = jnp.concatenate(weights, 0)
    small = exchange(small, EVERYWHERE)
    updated = call(merge_kernel, shape((16, 8, LANES), F32), [SMEM, VMEM])(coord_gain, small)
    place = jnp.stack([col, core[0], row]).astype(jnp.int32)

    groups = ROWS // 4
    projected = lambda count, size: [
        shape((ROWS, COLS, CH), BF16),
        shape((count, size, LANES), BF16),
    ]
    x, qkv, z = call(
        row_start_kernel,
        (*projected(8, 3 * 400 + 48), shape((2, 400, 4 * CH), BF16)),
        [SMEM] * 2 + [VMEM] * 7,
        [
            pltpu.VMEM((4 * CH, 3 * HEADS * LANES), BF16),
        ],
    )(
        place, updated, updated, sums, pair, pair_mask.T.astype(BF16), radial_pair, row_gain[None],
        weights,
    )

    qkv = exchange(qkv, ("z", "core"))
    all_xyz = updated[:, :, :15].reshape(16, 8, 5, 3).transpose(3, 0, 2, 1).reshape(3, LENGTH)
    new_coords = lax.dynamic_slice_in_dim(all_xyz, row * rows_n, rows_n, 1)
    new_state = call(
        node_kernel, shape((ROWS, node_width), F32), [SMEM] + [VMEM] * 4
    )(place, small, qkv, near, node_out_w)
    more_xyz = jnp.pad(all_xyz, ((0, 0), (0, OWNERS * BLOCK - HALF)))

    def gate(z, weight):
        return call(
            gate_kernel,
            shape((HEADS,) + z.shape[:2] + (LANES,), BF16),
            [VMEM] * 2,
            [pltpu.VMEM((4 * CH, HEADS * LANES), BF16)],
        )(z, weight)

    def bias(weight, head, place):
        first = core[0] * HALF + jnp.minimum(place, OWNERS - 1) * BLOCK
        tokens = lax.dynamic_slice_in_dim(more_xyz, first, BLOCK, 1).T
        return call(bias_kernel, shape((BLOCK, LENGTH), F32), [SMEM, VMEM, VMEM])(
            lax.dynamic_index_in_dim(weight, head, 1, keepdims=False), tokens, all_xyz
        )

    row_biases = bias(row_bias, lax.axis_index("z"), row)
    column_biases = bias(column_bias, lax.axis_index("x"), lax.axis_index(("y", "z")))
    qkv, *weights = lax.optimization_barrier(
        (qkv, column_query, column_key, column_value, row_out)
    )
    weights = jnp.concatenate(weights, 0)
    mixed, (new_state, new_coords), row_gates = tied_attention(
        COLS, qkv, core, row_biases, ("x", "y"), ("z", "core"),
        ((new_state, new_coords), gate(z, row_gate)),
    )
    x, qkv, z = call(
        column_start_kernel,
        (*projected(16, 3 * 208), shape((4, 208, 4 * CH), BF16)),
        [VMEM] * 6,
        [
            pltpu.VMEM((ROWS * COLS, CH), F32),
            pltpu.VMEM((HEADS * LANES, 4 * CH), BF16),
            pltpu.VMEM((4 * CH, 3 * HEADS * LANES), BF16),
        ],
    )(
        x, row_gates, mixed, pair_mask.astype(BF16), column_gain[None], weights,
    )
    mixed, _, column_gates = tied_attention(
        ROWS, exchange(qkv, ("x", "y")), core, column_biases, ("y", "z"), ("x", "y"),
        ((), gate(z, column_gate)),
    )
    pair_out = call(
        finish_kernel,
        shape((ROWS, COLS, CH), BF16),
        [VMEM] * 4,
        [
            pltpu.VMEM((ROWS * COLS, CH), F32),
            pltpu.VMEM((HEADS * LANES, 4 * CH), BF16),
        ],
    )(x, column_gates, mixed, column_out)
    return (pair_out, new_state, new_coords)


def solution(mesh):
    cube = Mesh(mesh.devices.reshape(4, 4, 4, 2), EVERYWHERE)
    row, col = ("x", "y"), ("z", "core")
    placed = (
        P(row, col, None), P(row, col), P(row, None), P(None, row), P(row, None), P(row),
    ) + (P(),) * 23
    return jax.shard_map(
        shards,
        mesh=cube,
        in_specs=placed,
        out_specs=(P(row, col, None), P(row, None), P(None, row)),
        check_vma=False,
    )
```

```python
import functools
import math

import jax
import jax.numpy as jnp
from jax import lax
from jax.experimental import pallas as pl
from jax.experimental.pallas import tpu as pltpu
from jax.sharding import Mesh
from jax.sharding import PartitionSpec as P

BF16 = jnp.bfloat16
F32 = jnp.float32
PRECISE = lax.Precision.HIGHEST
RADIAL_REACH = 24.0
NEGATIVE = -1e30
EVERYWHERE = ("x", "y", "z", "core")

VMEM = pl.BlockSpec(memory_space=pltpu.VMEM)
SMEM = pl.BlockSpec(memory_space=pltpu.SMEM)
MIB = 1024 * 1024

ROWS, COLS, CH, HEADS = 40, 80, 128, 4
LENGTH = 640
LANES = 128
SLOT = 32
BLOCK = 24
OWNERS = 14
HALF = LENGTH // 2


def call(kernel, out_shape, in_specs, scratch=(), limit=44):
    out_specs = jax.tree.map(lambda _: VMEM, out_shape)
    return pl.pallas_call(
        kernel,
        out_shape=out_shape,
        in_specs=in_specs,
        out_specs=out_specs,
        scratch_shapes=list(scratch),
        compiler_params=pltpu.CompilerParams(vmem_limit_bytes=limit * MIB),
    )


def shape(dims, dtype):
    return jax.ShapeDtypeStruct(dims, dtype)


def iota(dims, axis):
    return lax.broadcasted_iota(jnp.int32, dims, axis)


def dot(a, b):
    return jnp.dot(a, b, preferred_element_type=F32)


def dot32(a, b):
    return jnp.dot(a, b, preferred_element_type=F32, precision=PRECISE)


def length_of(square):
    square = square + 1e-06
    return square * lax.rsqrt(square)


def split(a):
    high = a.astype(BF16)
    return high, (a - high.astype(F32)).astype(BF16)


def split3(a):
    high, low = split(a)
    return high, low, (a - high.astype(F32) - low.astype(F32)).astype(BF16)


def graph_kernel(
    place_ref, xyz_ref, near_ref, way0_ref, way1_ref, pair_ref, neigh_ref, wq_ref, wk_ref, wv_ref,
    ep_ref, er_ref, small_ref, values_ref, q_ref, sums_ref,
):
    step = 8
    bins = 64
    lower = place_ref[1] == 1
    way0, way1 = way0_ref[...], way1_ref[...]
    far = jnp.concatenate([jnp.where(lower, way0, way1), jnp.where(lower, way1, way0)], 0)
    blank = jnp.zeros((64, LANES), F32)
    wq = jnp.concatenate([wq_ref[...] * 0.25, jnp.zeros((64, 64), F32)], 1)
    q_ref[...] = dot32(near_ref[...], jnp.concatenate([wq, blank], 0))
    wkv = jnp.concatenate([wk_ref[...], wv_ref[...]], 1)
    base = dot32(far, jnp.concatenate([wkv, blank], 0))
    far_xyz = [jnp.broadcast_to(far[:, 64 + c : 65 + c], (COLS, LANES)) for c in range(3)]
    lane = iota((1, LANES), 1)
    centers = (lane % bins).astype(F32) * (RADIAL_REACH / (bins - 1))
    width = bins / RADIAL_REACH
    of_lane, to_lane = iota((LANES, LANES), 0), iota((LANES, LANES), 1)
    to_value = (of_lane < 64) & (of_lane // 16 == (to_lane % 64) // 16)
    to_small = (of_lane < 64) & (of_lane // 16 == jnp.minimum(to_lane % 24 // 5, 3))
    head_sum = jnp.concatenate(
        [jnp.where(to_value, 1.0, 0.0), jnp.where(to_small, 1.0, 0.0)], 1
    ).astype(BF16)
    head_sum = jnp.concatenate([head_sum] * 3, 0)
    table_high, table_low = split(er_ref[...])
    table = jnp.concatenate([table_high, table_high, table_low, jnp.zeros_like(table_low)], 0)
    ones = jnp.ones((64, LANES), BF16)
    cell = iota((COLS, 64), 0) + place_ref[0]
    place = lane % 24
    slot = jnp.where(place < 20, place % 5, place - 15)

    def some(block, small):
        first = pl.multiple_of(block * step, step)
        offsets, bases, counts, queries = [], [], [], []
        neigh = neigh_ref[pl.ds(first, step), :]
        q_some = q_ref[pl.ds(first, step), :]
        for u in range(step):
            off = [far_xyz[c] - xyz_ref[c, first + u] for c in range(3)]
            spacing = length_of(off[0] * off[0] + off[1] * off[1] + off[2] * off[2])
            away = (spacing - centers) * width
            bases.append(jnp.exp(-(away * away)))
            offsets.append(off)
            counts.append(jnp.where(cell == neigh[u : u + 1, :], 1.0, 0.0).astype(BF16))
            queries.append(q_some[u : u + 1, :])
        cells = pair_ref[pl.ds(first, step)].reshape(step * COLS, CH)
        high, low = split(jnp.concatenate(bases, 0))
        bases = jnp.concatenate([jnp.where(lane < bins, high, low), high], 1)
        edge = dot(cells, ep_ref[...]) + dot(bases, table)
        count = dot(jnp.concatenate(counts, 0), ones)
        edges, products = [], []
        for u in range(step):
            one = edge[u * COLS : (u + 1) * COLS] + base
            edges.append(one)
            products.append(one * queries[u])
        scores = dot(jnp.concatenate(split3(jnp.concatenate(products, 0)), 1), head_sum)
        lines, sums = [], []
        for u in range(step):
            times = count[u * COLS : (u + 1) * COLS]
            score = scores[u * COLS : (u + 1) * COLS]
            both = []
            for part in (score[:, :LANES], score[:, LANES:]):
                part = jnp.where(times > 0.0, part, NEGATIVE)
                top = jnp.max(part, axis=0, keepdims=True)
                both.append((top, times * jnp.exp(part - top)))
            (_, for_value), (top, w) = both
            sums.append(jnp.sum(for_value * edges[u], axis=0, keepdims=True))
            entries = [top, jnp.sum(w, axis=0, keepdims=True)]
            entries += [jnp.sum(w * offsets[u][c], axis=0, keepdims=True) for c in range(3)]
            entries += [xyz_ref[c, first + u] for c in range(3)]
            line = jnp.zeros((1, LANES), F32)
            for at, entry in enumerate(entries):
                line = jnp.where(slot == at, entry, line)
            lines.append(line)
        sums_ref[pl.ds(first, step), :] = jnp.concatenate(sums, 0)
        return jnp.where(lane // 24 == block, jnp.concatenate(lines, 0), small)

    small = lax.fori_loop(0, ROWS // step, some, jnp.zeros((step, LANES), F32), unroll=True)
    small_ref[...] = jnp.broadcast_to(small[None], small_ref.shape)
    sums = sums_ref[...]
    turned = pltpu.roll(sums, 64, 1)
    high = turned.astype(BF16).astype(F32)
    low = sums - sums.astype(BF16).astype(F32)
    values = jnp.where(lane < 64, high, low)
    values_ref[...] = jnp.concatenate([values, jnp.zeros((8, LANES), F32)], 0).astype(BF16)


def merge_kernel(gain_ref, parts_ref, out_ref):
    of_lane, to_lane = iota((LANES, LANES), 0), iota((LANES, LANES), 1)
    first = jnp.where(to_lane < 120, to_lane // 24 * 24, 0)
    home = first + jnp.minimum(to_lane % 24 // 5, 3) * 5
    to_top = jnp.where(of_lane == home, 1.0, 0.0).astype(BF16)
    to_total = jnp.where(of_lane == home + 1, 1.0, 0.0)
    start = to_lane // 3 * 24
    gain = jnp.zeros((LANES, LANES), F32)
    for head in range(4):
        at = (of_lane == start + head * 5 + 2 + to_lane % 3) & (to_lane < 15)
        gain = jnp.where(at, gain_ref[head], gain)
    to_old = jnp.where((of_lane == start + 20 + to_lane % 3) & (to_lane < 15), 1.0, 0.0)
    parts = parts_ref[...].reshape(128 * 8, LANES)
    tops = dot(jnp.concatenate(split3(parts), 1), jnp.concatenate([to_top] * 3, 0))
    merged, old = [], []
    for row in range(16):
        some = [slice((row * 8 + p) * 8, (row * 8 + p + 1) * 8) for p in range(8)]
        highest = functools.reduce(jnp.maximum, [tops[at] for at in some])
        merged.append(sum(jnp.exp(tops[at] - highest) * parts[at] for at in some))
        old.append(parts[some[0]])
    merged = jnp.concatenate(merged, 0)
    ratio = merged / dot32(merged, to_total)
    new = dot32(jnp.concatenate(old, 0), to_old) + dot32(ratio, gain)
    out_ref[...] = new.reshape(16, 8, LANES)


def node_kernel(place_ref, parts_ref, sent_ref, near_ref, wo_ref, out_ref):
    lane = iota((8, LANES), 1)
    of_lane, to_lane = iota((LANES, LANES), 0), iota((LANES, LANES), 1)
    parts = [parts_ref[place_ref[2] * 8 + p] for p in range(8)]
    values = [sent_ref[p, sent_ref.shape[1] - 48 :, :].astype(F32) for p in range(8)]
    values = [value + pltpu.roll(value, 64, 1) for value in values]
    stacked = jnp.concatenate(parts, 0)
    attended = []
    for g in range(5):
        home = g * 24 + (to_lane % 64) // 16 * 5 + to_lane // 64
        both = dot32(stacked, jnp.where(of_lane == home, 1.0, 0.0))
        tops = [both[p * 8 : (p + 1) * 8] for p in range(8)]
        highest = functools.reduce(jnp.maximum, tops)
        above, below = 0.0, 0.0
        for p in range(8):
            scale = jnp.exp(tops[p] - highest)
            above = above + scale * values[p][g * 8 : (g + 1) * 8]
            below = below + scale * pltpu.roll(tops[p], 64, 1)
        attended.append(jnp.where(lane < 64, above / jnp.where(lane < 64, below, 1.0), 0.0))
    attended = jnp.concatenate(attended, 0)[:, :64]
    out_ref[...] = near_ref[...][:, :64] + dot32(attended, wo_ref[...])


def widen(weight, wide_ref, column):
    weight = weight.astype(F32)
    lane = iota((CH, LANES), 1)
    for h in range(HEADS):
        for i in range(4):
            turned = pltpu.roll(weight, ((i - h) * SLOT) % LANES, 1) if i != h else weight
            wide_ref[i * CH : (i + 1) * CH, column + h * LANES : column + (h + 1) * LANES] = (
                jnp.where(lane // SLOT == i, turned, 0.0).astype(BF16)
            )


def widen_out(weight, wide_ref):
    wide_ref[...] = jnp.zeros_like(wide_ref)
    for h in range(HEADS):
        for i in range(4):
            wide_ref[
                h * LANES + i * SLOT : h * LANES + (i + 1) * SLOT, i * CH : (i + 1) * CH
            ] = weight[h * SLOT : (h + 1) * SLOT, :]


def normed(rounded, norm_gain):
    mean_of = jnp.full((CH, LANES), 1.0 / CH, BF16)
    centered = rounded.astype(F32) - dot(rounded, mean_of)
    high, low = split(centered * centered)
    spread = dot(jnp.concatenate([high, low], 1), jnp.concatenate([mean_of, mean_of], 0))
    return centered * lax.rsqrt(spread + 1e-05) * norm_gain


def spread_mask(mask, group):
    n = mask.shape[1]
    pick = iota((n, LANES), 0) == 4 * group + iota((n, LANES), 1) // SLOT
    return dot(mask, jnp.where(pick, 1.0, 0.0).astype(BF16))


def put_projections(z, mask, wide_ref, put):
    scales = (1.0 / math.sqrt(SLOT), 1.0 / math.sqrt(LENGTH))
    for matrix in range(3):
        wide = HEADS * LANES
        out = dot(z, wide_ref[:, matrix * wide : (matrix + 1) * wide])
        for h in range(HEADS):
            one = out[:, h * LANES : (h + 1) * LANES]
            if matrix < 2:
                one = one * mask * scales[matrix]
            put(matrix, h, one)


def gate_kernel(z_ref, weight_ref, gate_ref, wide_ref):
    widen(weight_ref[...], wide_ref, 0)
    for block in range(z_ref.shape[0]):
        out = jax.nn.sigmoid(dot(z_ref[block], wide_ref[...]))
        for h in range(HEADS):
            gate_ref[h, block] = out[:, h * LANES : (h + 1) * LANES].astype(BF16)


def row_start_kernel(
    place_ref, xyz_ref, new_ref, sums_ref, pair_ref, mask_ref, radial_ref, gain_ref, weights_ref,
    x_ref, qkv_ref, z_ref, wide_ref,
):
    bins = 64
    for at in range(3):
        widen(weights_ref[at * CH : (at + 1) * CH, :], wide_ref, at * HEADS * LANES)
    far = [new_ref[place_ref[0] * 2 + half] for half in range(2)]
    far_xyz = [
        jnp.concatenate(
            [
                jnp.broadcast_to(part[:, g * 3 + c : g * 3 + c + 1], (8, LANES))
                for part in far
                for g in range(5)
            ],
            0,
        )
        for c in range(3)
    ]
    row = place_ref[2]
    lane = iota((1, LANES), 1)
    centers = (lane % bins).astype(F32) * (RADIAL_REACH / (bins - 1))
    width = bins / RADIAL_REACH
    table = radial_ref[...]
    blank = jnp.zeros_like(table)
    table = jnp.concatenate(
        [jnp.concatenate([table, blank], 1), jnp.concatenate([blank, table], 1)], 0
    )
    table_high, table_low = split(table)
    table = jnp.concatenate([table_high, table_low, table_high], 0)
    norm_gain = gain_ref[...]

    together = 2
    size = ROWS // 8 * COLS

    def some(step, carry):
        bases, rows = [], []
        for at in range(2 * together):
            n = (step * together * 2 + at) * 2
            off = [
                far_xyz[c]
                - jnp.where(
                    lane < bins,
                    xyz_ref[row, n & 7, (n >> 3) * 3 + c],
                    xyz_ref[row, (n + 1) & 7, ((n + 1) >> 3) * 3 + c],
                )
                for c in range(3)
            ]
            spacing = length_of(off[0] * off[0] + off[1] * off[1] + off[2] * off[2])
            away = (spacing - centers) * width
            bases.append(jnp.exp(-(away * away)))
        high, low = split(jnp.concatenate(bases, 0))
        added = dot(jnp.concatenate([high, high, low], 1), table)
        for i in range(4 * together):
            at = (i // 2) * COLS
            n = step * together * 4 + i
            part = added[at : at + COLS, (i % 2) * CH : (i % 2 + 1) * CH]
            rows.append((pair_ref[n].astype(F32) + part).astype(BF16))
            x_ref[n] = rows[-1]
        z = normed(jnp.concatenate(rows, 0), norm_gain).astype(BF16)
        for i in range(4 * together):
            at = (step * together + i // 4) * COLS
            half, at = at // size, at % size
            z_ref[half, pl.ds(pl.multiple_of(at, COLS), COLS), (i % 4) * CH : (i % 4 + 1) * CH] = z[
                i * COLS : (i + 1) * COLS
            ]
        return carry

    groups = ROWS // 4
    lax.fori_loop(0, groups // together, some, 0, unroll=True)
    for s in range(2):
        for h in range(HEADS):
            qkv_ref[h * 2 + s, 3 * size :] = sums_ref[...]
        mask = jnp.concatenate(
            [spread_mask(mask_ref[...], s * (groups // 2) + g) for g in range(groups // 2)], 0
        )

        def put(matrix, h, one):
            qkv_ref[h * 2 + s, matrix * size : (matrix + 1) * size] = one.astype(BF16)

        put_projections(z_ref[s], mask, wide_ref, put)


def gathered(parts_ref, which, g, across):
    count = parts_ref.shape[0]
    if across == COLS:
        at = (which * 5 + g) * across
        return jnp.concatenate([parts_ref[p, at : at + across, :] for p in range(count)], 0)
    size = parts_ref.shape[1] // 3
    return jnp.concatenate(
        [
            parts_ref[p, which * size : (which + 1) * size].astype(F32)[
                g * across : (g + 1) * across
            ]
            for p in range(count)
        ],
        0,
    ).astype(BF16)


def logits_kernel(across, core_ref, qkv_ref, own_ref, other_ref, q_ref, k_ref, sum_ref):
    for g in range(5):
        q_ref[:, g * LANES : (g + 1) * LANES] = gathered(qkv_ref, 0, g, across)
        k_ref[:, g * LANES : (g + 1) * LANES] = gathered(qkv_ref, 1, g, across)
    rows = 128
    for m in range(LENGTH // rows):
        sum_ref[m * rows : (m + 1) * rows, :] = lax.dot_general(
            q_ref[m * rows : (m + 1) * rows, :],
            k_ref[...],
            (((1,), (1,)), ((), ())),
            preferred_element_type=F32,
        )
    core = core_ref[0]
    own_ref[...] = sum_ref[pl.ds(pl.multiple_of(core * HALF, HALF), HALF), :]
    other_ref[...] = sum_ref[pl.ds(pl.multiple_of((1 - core) * HALF, HALF), HALF), :].astype(BF16)


def join_kernel(own_ref, other_ref, out_ref):
    out_ref[OWNERS:] = jnp.zeros((out_ref.shape[0] - OWNERS, BLOCK, LENGTH), BF16)
    total = own_ref[...] + other_ref[...].astype(F32)
    spare = jnp.zeros((OWNERS * BLOCK - HALF, LENGTH), F32)
    total = jnp.concatenate([total, spare], 0)
    for m in range(OWNERS):
        out_ref[m] = total[m * BLOCK : (m + 1) * BLOCK].astype(BF16)


def turned_dot(a, b):
    return sum(
        lax.dot_general(a, part, (((1,), (1,)), ((), ())), preferred_element_type=F32)
        for part in split3(b)
    )


def places_kernel(new_ref, out_ref):
    flat = new_ref[...].reshape(LANES, LANES)
    sides = []
    for g in range(5):
        pick = (iota((8, LANES), 1) == iota((8, LANES), 0) + 3 * g) & (iota((8, LANES), 0) < 3)
        sides.append(turned_dot(jnp.where(pick, 1.0, 0.0).astype(BF16), flat))
    parts = jnp.concatenate(split3(jnp.concatenate(sides, 1)), 0)
    at, token = iota((LENGTH, LENGTH), 0), iota((LENGTH, LENGTH), 1)
    target = (at & 127) // 8 * ROWS + at // LANES * 8 + (at & 7)
    moved = dot(parts, jnp.where(target == token, 1.0, 0.0).astype(BF16))
    out_ref[...] = moved[:8] + moved[8:16] + moved[16:]


def bias_kernel(place_ref, weight_ref, far_ref, out_ref):
    bins = 64
    far = far_ref[...]
    pick = iota((BLOCK, LENGTH), 1) == iota((BLOCK, LENGTH), 0) + place_ref[1]
    near = turned_dot(jnp.where(pick, 1.0, 0.0).astype(BF16), far)
    square = jnp.zeros((BLOCK, LENGTH), F32)
    for c in range(3):
        off = near[:, c : c + 1] - far[c : c + 1, :]
        square = square + off * off
    width = bins / RADIAL_REACH
    spacing = length_of(square) * width

    def some(at, total):
        for u in range(8):
            b = at * 8 + u
            away = spacing - b.astype(F32) * (width * RADIAL_REACH / (bins - 1))
            total = total + weight_ref[b, place_ref[0]] * jnp.exp(-(away * away))
        return total

    out_ref[...] = lax.fori_loop(0, bins // 8, some, jnp.zeros((BLOCK, LENGTH), F32))


def softmax_kernel(parts_ref, bias_ref, out_ref):
    count = parts_ref.shape[0]
    logits = bias_ref[...]
    for p in range(count):
        logits = logits + parts_ref[p].astype(F32)
    scaled = jnp.exp(logits - jnp.max(logits, axis=-1, keepdims=True))
    weights = (scaled / jnp.sum(scaled, axis=-1, keepdims=True)).astype(BF16)
    for p in range(count):
        out_ref[p] = weights


def mix_kernel(across, core_ref, own_ref, other_ref, parts_ref, out_ref, a_ref, v_ref):
    core = core_ref[0]
    for ref, half in ((own_ref, core), (other_ref, 1 - core)):
        rows = jnp.concatenate([ref[m].astype(F32) for m in range(OWNERS)], 0)[:HALF]
        a_ref[pl.ds(pl.multiple_of(half * HALF, HALF), HALF), :] = rows.astype(BF16)
    for g in range(5):
        v_ref[:, g * LANES : (g + 1) * LANES] = gathered(parts_ref, 2, g, across)
    rows = 160
    for m in range(LENGTH // rows):
        mixed = dot(a_ref[m * rows : (m + 1) * rows, :], v_ref[...])
        for p in range(rows // across):
            pieces = [
                mixed[p * across : (p + 1) * across, g * LANES : (g + 1) * LANES]
                for g in range(5)
            ]
            spare = out_ref.shape[1] - 5 * across
            if spare:
                pieces.append(jnp.zeros((spare, LANES), F32))
            out_ref[m * (rows // across) + p] = jnp.concatenate(pieces, 0).astype(BF16)


def column_start_kernel(
    x_ref, gate_ref, mixed_ref, mask_ref, gain_ref, weights_ref,
    new_ref, qkv_ref, turned_ref, z_ref, wide_out_ref, wide_ref,
):
    widen_out(weights_ref[3 * CH :, :], wide_out_ref)
    for at in range(3):
        widen(weights_ref[at * CH : (at + 1) * CH, :], wide_ref, at * HEADS * LANES)
    norm_gain = gain_ref[...]
    for s in range(2):
        gated = jnp.concatenate(
            [
                (gate_ref[h, s].astype(F32) * mixed_ref[h * 2 + s].astype(F32)).astype(BF16)
                for h in range(HEADS)
            ],
            1,
        )
        update = dot(gated, wide_out_ref[...])
        for g in range(5):
            rows = []
            for i in range(4):
                n = (s * 5 + g) * 4 + i
                part = update[g * COLS : (g + 1) * COLS, i * CH : (i + 1) * CH]
                rows.append((x_ref[n].astype(F32) + part).astype(BF16))
                new_ref[n] = rows[-1]
            z = normed(jnp.concatenate(rows, 0), norm_gain)
            first = (s * 5 + g) * 4 * COLS
            z_ref[first : first + 4 * COLS, :] = z
    for chunk in range(4):
        pieces, masks = [], []
        for g in range(5):
            column = (chunk * 5 + g) * 4
            pieces.append(
                jnp.concatenate(
                    [z_ref[pl.ds(column + i, ROWS, stride=COLS), :] for i in range(4)], 1
                )
            )
            masks.append(spread_mask(mask_ref[...], chunk * 5 + g))

        size = qkv_ref.shape[1] // 3
        z = jnp.concatenate(pieces, 0)
        spare = size - z.shape[0]
        z = jnp.concatenate([z, jnp.zeros((spare, z.shape[1]), F32)], 0).astype(BF16)
        turned_ref[chunk] = z
        mask = jnp.concatenate(masks + [jnp.zeros((spare, LANES), F32)], 0)

        def put(matrix, h, one):
            qkv_ref[h * 4 + chunk, matrix * size : (matrix + 1) * size] = one.astype(BF16)

        put_projections(z, mask, wide_ref, put)


def finish_kernel(x_ref, gate_ref, mixed_ref, wo_ref, out_ref, turned_ref, wide_out_ref):
    widen_out(wo_ref[...], wide_out_ref)
    for chunk in range(4):
        gated = jnp.concatenate(
            [
                gate_ref[h, chunk].astype(F32) * mixed_ref[h * 4 + chunk].astype(F32)
                for h in range(HEADS)
            ],
            1,
        ).astype(BF16)
        update = dot(gated, wide_out_ref[...])
        for g in range(5):
            for i in range(4):
                column = (chunk * 5 + g) * 4 + i
                turned_ref[pl.ds(column, ROWS, stride=COLS), :] = update[
                    g * ROWS : (g + 1) * ROWS, i * CH : (i + 1) * CH
                ]
    for n in range(ROWS):
        out_ref[n] = (x_ref[n].astype(F32) + turned_ref[n * COLS : (n + 1) * COLS, :]).astype(BF16)


def exchange(parts, axes):
    return lax.all_to_all(parts, axes, split_axis=0, concat_axis=0, tiled=True)


def swap_cores(x):
    return lax.ppermute(x, "core", [(0, 1), (1, 0)])


def column_tokens(mine, cols_n):
    device = lambda r, c: r * cols_n + c
    half = cols_n
    rows_n = 2 * cols_n
    ways = []
    for flip in (0, 1):
        pairs = [
            (device(r, c), device(c + half * ((r % 2) ^ flip), r // 2))
            for r in range(rows_n)
            for c in range(cols_n)
        ]
        ways.append(lax.ppermute(mine, EVERYWHERE, pairs))
    return ways


def tied_attention(across, qkv, core, bias, sum_axes, pass_axes, beside):
    own, other = call(
        functools.partial(logits_kernel, across),
        (shape((HALF, LENGTH), F32), shape((HALF, LENGTH), BF16)),
        [SMEM, VMEM],
        [
            pltpu.VMEM((LENGTH, 5 * LANES), BF16),
            pltpu.VMEM((LENGTH, 5 * LANES), BF16),
            pltpu.VMEM((LENGTH, LENGTH), F32),
        ],
    )(core, qkv)
    parts = call(join_kernel, shape((16, BLOCK, LENGTH), BF16), [VMEM] * 2)(own, swap_cores(other))
    parts, beside = lax.optimization_barrier((exchange(parts, sum_axes), beside))
    weights = call(softmax_kernel, shape((16, BLOCK, LENGTH), BF16), [VMEM] * 2)(
        parts, bias
    )
    own = exchange(weights, sum_axes)
    other = swap_cores(own)
    mixed = call(
        functools.partial(mix_kernel, across),
        shape((qkv.shape[0], 5 * across + 5 * across % 16, LANES), BF16),
        [SMEM, VMEM, VMEM, VMEM],
        [pltpu.VMEM((LENGTH, LENGTH), BF16), pltpu.VMEM((LENGTH, 5 * LANES), BF16)],
    )(core, own, other, qkv)
    return exchange(mixed, pass_axes), beside


def shards(
    pair, pair_mask, node_state, coords, neighbours, atom_type, type_table, node_query, node_key,
    node_value, edge_pair, edge_radial, node_out_w, coord_gain, radial_pair, row_gain, row_query,
    row_key, row_value, row_gate, row_out, row_bias, column_gain, column_query, column_key,
    column_value, column_gate, column_out, column_bias,
):
    rows_n, cols_n, channels = pair.shape
    row, col = lax.axis_index(("x", "y")), lax.axis_index(("z", "core"))
    core = lax.axis_index("core")[None].astype(jnp.int32)
    node_width = node_state.shape[1]
    onehot = (atom_type[:, None] == jnp.arange(type_table.shape[0], dtype=jnp.int32)[None, :])
    features = node_state + jnp.dot(onehot.astype(F32), type_table, precision=PRECISE)
    spare = LANES - node_width
    near = jnp.concatenate(
        [features, coords.T, jnp.zeros((rows_n, spare - coords.shape[0]), F32)], 1
    )
    ways = column_tokens(near, 8)
    place = jnp.stack([col * cols_n, (row < 8).astype(jnp.int32)]).astype(jnp.int32)
    remote = (pair, neighbours, node_query, node_key, node_value, edge_pair, edge_radial)
    small, sums = call(
        graph_kernel,
        (shape((128, 8, LANES), F32), shape((48, LANES), BF16)),
        [SMEM] * 2 + [VMEM] * 10,
        [pltpu.VMEM((ROWS, LANES), F32)] * 2,
        limit=60,
    )(place, coords, near, *ways, *remote)
    small, *weights = lax.optimization_barrier((small, row_query, row_key, row_value))
    weights = jnp.concatenate(weights, 0)
    small = exchange(small, EVERYWHERE)
    updated = call(merge_kernel, shape((16, 8, LANES), F32), [SMEM, VMEM])(coord_gain, small)
    place = jnp.stack([col, core[0], row]).astype(jnp.int32)

    groups = ROWS // 4
    projected = lambda count, size: [
        shape((ROWS, COLS, CH), BF16),
        shape((count, size, LANES), BF16),
    ]
    x, qkv, z = call(
        row_start_kernel,
        (*projected(8, 3 * 400 + 48), shape((2, 400, 4 * CH), BF16)),
        [SMEM] * 2 + [VMEM] * 7,
        [
            pltpu.VMEM((4 * CH, 3 * HEADS * LANES), BF16),
        ],
    )(
        place, updated, updated, sums, pair, pair_mask.T.astype(BF16), radial_pair, row_gain[None],
        weights,
    )

    qkv = exchange(qkv, ("z", "core"))
    all_xyz = call(places_kernel, shape((8, LENGTH), F32), [VMEM])(updated)
    new_coords = lax.dynamic_slice(all_xyz, (0, row * rows_n), (3, rows_n))
    new_state = call(
        node_kernel, shape((ROWS, node_width), F32), [SMEM] + [VMEM] * 4
    )(place, small, qkv, near, node_out_w)
    def gate(z, weight):
        return call(
            gate_kernel,
            shape((HEADS,) + z.shape[:2] + (LANES,), BF16),
            [VMEM] * 2,
            [pltpu.VMEM((4 * CH, HEADS * LANES), BF16)],
        )(z, weight)

    def bias(weight, head, owner):
        first = core[0] * HALF + jnp.minimum(owner, OWNERS - 1) * BLOCK
        return call(bias_kernel, shape((BLOCK, LENGTH), F32), [SMEM, SMEM, VMEM])(
            jnp.stack([head, first]).astype(jnp.int32), weight, all_xyz
        )

    row_biases = bias(row_bias, lax.axis_index("z"), row)
    column_biases = bias(column_bias, lax.axis_index("x"), lax.axis_index(("y", "z")))
    qkv, *weights = lax.optimization_barrier(
        (qkv, column_query, column_key, column_value, row_out)
    )
    weights = jnp.concatenate(weights, 0)
    mixed, (new_state, new_coords, row_gates) = tied_attention(
        COLS, qkv, core, row_biases, ("x", "y"), ("z", "core"),
        (new_state, new_coords, gate(z, row_gate)),
    )
    x, qkv, z = call(
        column_start_kernel,
        (*projected(16, 3 * 208), shape((4, 208, 4 * CH), BF16)),
        [VMEM] * 6,
        [
            pltpu.VMEM((ROWS * COLS, CH), F32),
            pltpu.VMEM((HEADS * LANES, 4 * CH), BF16),
            pltpu.VMEM((4 * CH, 3 * HEADS * LANES), BF16),
        ],
    )(
        x, row_gates, mixed, pair_mask.astype(BF16), column_gain[None], weights,
    )
    mixed, column_gates = tied_attention(
        ROWS, exchange(qkv, ("x", "y")), core, column_biases, ("y", "z"), ("x", "y"),
        gate(z, column_gate),
    )
    pair_out = call(
        finish_kernel,
        shape((ROWS, COLS, CH), BF16),
        [VMEM] * 4,
        [
            pltpu.VMEM((ROWS * COLS, CH), F32),
            pltpu.VMEM((HEADS * LANES, 4 * CH), BF16),
        ],
    )(x, column_gates, mixed, column_out)
    return (pair_out, new_state, new_coords)


def solution(mesh):
    cube = Mesh(mesh.devices.reshape(4, 4, 4, 2), EVERYWHERE)
    row, col = ("x", "y"), ("z", "core")
    placed = (
        P(row, col, None), P(row, col), P(row, None), P(None, row), P(row, None), P(row),
    ) + (P(),) * 23
    return jax.shard_map(
        shards,
        mesh=cube,
        in_specs=placed,
        out_specs=(P(row, col, None), P(row, None), P(None, row)),
        check_vma=False,
    )
```

```python
import functools
import math

import jax
import jax.numpy as jnp
from jax import lax
from jax.experimental import pallas as pl
from jax.experimental.pallas import tpu as pltpu
from jax.sharding import Mesh
from jax.sharding import PartitionSpec as P

BF16 = jnp.bfloat16
F32 = jnp.float32
PRECISE = lax.Precision.HIGHEST
RADIAL_REACH = 24.0
NEGATIVE = -1e30
EVERYWHERE = ("x", "y", "z", "core")

VMEM = pl.BlockSpec(memory_space=pltpu.VMEM)
SMEM = pl.BlockSpec(memory_space=pltpu.SMEM)
MIB = 1024 * 1024

ROWS, COLS, CH, HEADS = 40, 80, 128, 4
LENGTH = 640
LANES = 128
SLOT = 32
BLOCK = 24
OWNERS = 14
HALF = LENGTH // 2


def call(kernel, out_shape, in_specs, scratch=(), limit=44):
    out_specs = jax.tree.map(lambda _: VMEM, out_shape)
    return pl.pallas_call(
        kernel,
        out_shape=out_shape,
        in_specs=in_specs,
        out_specs=out_specs,
        scratch_shapes=list(scratch),
        compiler_params=pltpu.CompilerParams(vmem_limit_bytes=limit * MIB),
    )


def shape(dims, dtype):
    return jax.ShapeDtypeStruct(dims, dtype)


def iota(dims, axis):
    return lax.broadcasted_iota(jnp.int32, dims, axis)


def dot(a, b):
    return jnp.dot(a, b, preferred_element_type=F32)


def dot32(a, b):
    return jnp.dot(a, b, preferred_element_type=F32, precision=PRECISE)


def length_of(square):
    square = square + 1e-06
    return square * lax.rsqrt(square)


def split(a):
    high = a.astype(BF16)
    return high, (a - high.astype(F32)).astype(BF16)


def split3(a):
    high, low = split(a)
    return high, low, (a - high.astype(F32) - low.astype(F32)).astype(BF16)


def graph_kernel(
    place_ref, xyz_ref, near_ref, way0_ref, way1_ref, pair_ref, neigh_ref, wq_ref, wk_ref, wv_ref,
    ep_ref, er_ref, small_ref, values_ref, q_ref, sums_ref,
):
    step = 8
    bins = 64
    lower = place_ref[1] == 1
    way0, way1 = way0_ref[...], way1_ref[...]
    far = jnp.concatenate([jnp.where(lower, way0, way1), jnp.where(lower, way1, way0)], 0)
    blank = jnp.zeros((64, LANES), F32)
    wq = jnp.concatenate([wq_ref[...] * 0.25, jnp.zeros((64, 64), F32)], 1)
    q_ref[...] = dot32(near_ref[...], jnp.concatenate([wq, blank], 0))
    wkv = jnp.concatenate([wk_ref[...], wv_ref[...]], 1)
    base = dot32(far, jnp.concatenate([wkv, blank], 0))
    far_xyz = [jnp.broadcast_to(far[:, 64 + c : 65 + c], (COLS, LANES)) for c in range(3)]
    lane = iota((1, LANES), 1)
    centers = (lane % bins).astype(F32) * (RADIAL_REACH / (bins - 1))
    width = bins / RADIAL_REACH
    of_lane, to_lane = iota((LANES, LANES), 0), iota((LANES, LANES), 1)
    to_value = (of_lane < 64) & (of_lane // 16 == (to_lane % 64) // 16)
    to_small = (of_lane < 64) & (of_lane // 16 == jnp.minimum(to_lane % 24 // 5, 3))
    head_sum = jnp.concatenate(
        [jnp.where(to_value, 1.0, 0.0), jnp.where(to_small, 1.0, 0.0)], 1
    ).astype(BF16)
    head_sum = jnp.concatenate([head_sum] * 3, 0)
    table_high, table_low = split(er_ref[...])
    table = jnp.concatenate([table_high, table_high, table_low, jnp.zeros_like(table_low)], 0)
    ones = jnp.ones((64, LANES), BF16)
    cell = iota((COLS, 64), 0) + place_ref[0]
    place = lane % 24
    slot = jnp.where(place < 20, place % 5, place - 15)

    def some(block, small):
        first = pl.multiple_of(block * step, step)
        offsets, bases, counts, queries = [], [], [], []
        neigh = neigh_ref[pl.ds(first, step), :]
        q_some = q_ref[pl.ds(first, step), :]
        for u in range(step):
            off = [far_xyz[c] - xyz_ref[c, first + u] for c in range(3)]
            spacing = length_of(off[0] * off[0] + off[1] * off[1] + off[2] * off[2])
            away = (spacing - centers) * width
            bases.append(jnp.exp(-(away * away)))
            offsets.append(off)
            counts.append(jnp.where(cell == neigh[u : u + 1, :], 1.0, 0.0).astype(BF16))
            queries.append(q_some[u : u + 1, :])
        cells = pair_ref[pl.ds(first, step)].reshape(step * COLS, CH)
        high, low = split(jnp.concatenate(bases, 0))
        bases = jnp.concatenate([jnp.where(lane < bins, high, low), high], 1)
        edge = dot(cells, ep_ref[...]) + dot(bases, table)
        count = dot(jnp.concatenate(counts, 0), ones)
        edges, products = [], []
        for u in range(step):
            one = edge[u * COLS : (u + 1) * COLS] + base
            edges.append(one)
            products.append(one * queries[u])
        scores = dot(jnp.concatenate(split3(jnp.concatenate(products, 0)), 1), head_sum)
        lines, sums = [], []
        for u in range(step):
            times = count[u * COLS : (u + 1) * COLS]
            score = scores[u * COLS : (u + 1) * COLS]
            both = []
            for part in (score[:, :LANES], score[:, LANES:]):
                part = jnp.where(times > 0.0, part, NEGATIVE)
                top = jnp.max(part, axis=0, keepdims=True)
                both.append((top, times * jnp.exp(part - top)))
            (_, for_value), (top, w) = both
            sums.append(jnp.sum(for_value * edges[u], axis=0, keepdims=True))
            entries = [top, jnp.sum(w, axis=0, keepdims=True)]
            entries += [jnp.sum(w * offsets[u][c], axis=0, keepdims=True) for c in range(3)]
            entries += [xyz_ref[c, first + u] for c in range(3)]
            line = jnp.zeros((1, LANES), F32)
            for at, entry in enumerate(entries):
                line = jnp.where(slot == at, entry, line)
            lines.append(line)
        sums_ref[pl.ds(first, step), :] = jnp.concatenate(sums, 0)
        return jnp.where(lane // 24 == block, jnp.concatenate(lines, 0), small)

    small = lax.fori_loop(0, ROWS // step, some, jnp.zeros((step, LANES), F32), unroll=True)
    small_ref[...] = jnp.broadcast_to(small[None], small_ref.shape)
    sums = sums_ref[...]
    turned = pltpu.roll(sums, 64, 1)
    high = turned.astype(BF16).astype(F32)
    low = sums - sums.astype(BF16).astype(F32)
    values = jnp.where(lane < 64, high, low)
    values_ref[...] = jnp.concatenate([values, jnp.zeros((8, LANES), F32)], 0).astype(BF16)


def merge_kernel(gain_ref, parts_ref, out_ref):
    of_lane, to_lane = iota((LANES, LANES), 0), iota((LANES, LANES), 1)
    first = jnp.where(to_lane < 120, to_lane // 24 * 24, 0)
    home = first + jnp.minimum(to_lane % 24 // 5, 3) * 5
    to_top = jnp.where(of_lane == home, 1.0, 0.0).astype(BF16)
    to_total = jnp.where(of_lane == home + 1, 1.0, 0.0)
    start = to_lane // 3 * 24
    gain = jnp.zeros((LANES, LANES), F32)
    for head in range(4):
        at = (of_lane == start + head * 5 + 2 + to_lane % 3) & (to_lane < 15)
        gain = jnp.where(at, gain_ref[head], gain)
    to_old = jnp.where((of_lane == start + 20 + to_lane % 3) & (to_lane < 15), 1.0, 0.0)
    parts = parts_ref[...].reshape(128 * 8, LANES)
    tops = dot(jnp.concatenate(split3(parts), 1), jnp.concatenate([to_top] * 3, 0))
    merged, old = [], []
    for row in range(16):
        some = [slice((row * 8 + p) * 8, (row * 8 + p + 1) * 8) for p in range(8)]
        highest = functools.reduce(jnp.maximum, [tops[at] for at in some])
        merged.append(sum(jnp.exp(tops[at] - highest) * parts[at] for at in some))
        old.append(parts[some[0]])
    merged = jnp.concatenate(merged, 0)
    ratio = merged / dot32(merged, to_total)
    new = dot32(jnp.concatenate(old, 0), to_old) + dot32(ratio, gain)
    out_ref[...] = new.reshape(16, 8, LANES)


def node_kernel(place_ref, parts_ref, sent_ref, near_ref, wo_ref, out_ref):
    lane = iota((8, LANES), 1)
    of_lane, to_lane = iota((LANES, LANES), 0), iota((LANES, LANES), 1)
    parts = [parts_ref[place_ref[2] * 8 + p] for p in range(8)]
    values = [sent_ref[p, sent_ref.shape[1] - 48 :, :].astype(F32) for p in range(8)]
    values = [value + pltpu.roll(value, 64, 1) for value in values]
    stacked = jnp.concatenate(parts, 0)
    attended = []
    for g in range(5):
        home = g * 24 + (to_lane % 64) // 16 * 5 + to_lane // 64
        both = dot32(stacked, jnp.where(of_lane == home, 1.0, 0.0))
        tops = [both[p * 8 : (p + 1) * 8] for p in range(8)]
        highest = functools.reduce(jnp.maximum, tops)
        above, below = 0.0, 0.0
        for p in range(8):
            scale = jnp.exp(tops[p] - highest)
            above = above + scale * values[p][g * 8 : (g + 1) * 8]
            below = below + scale * pltpu.roll(tops[p], 64, 1)
        attended.append(jnp.where(lane < 64, above / jnp.where(lane < 64, below, 1.0), 0.0))
    attended = jnp.concatenate(attended, 0)[:, :64]
    out_ref[...] = near_ref[...][:, :64] + dot32(attended, wo_ref[...])


def widen(weight, wide_ref, column):
    weight = weight.astype(F32)
    lane = iota((CH, LANES), 1)
    for h in range(HEADS):
        for i in range(4):
            turned = pltpu.roll(weight, ((i - h) * SLOT) % LANES, 1) if i != h else weight
            wide_ref[i * CH : (i + 1) * CH, column + h * LANES : column + (h + 1) * LANES] = (
                jnp.where(lane // SLOT == i, turned, 0.0).astype(BF16)
            )


def widen_out(weight, wide_ref):
    wide_ref[...] = jnp.zeros_like(wide_ref)
    for h in range(HEADS):
        for i in range(4):
            wide_ref[
                h * LANES + i * SLOT : h * LANES + (i + 1) * SLOT, i * CH : (i + 1) * CH
            ] = weight[h * SLOT : (h + 1) * SLOT, :]


def normed(rounded, norm_gain):
    mean_of = jnp.full((CH, LANES), 1.0 / CH, BF16)
    centered = rounded.astype(F32) - dot(rounded, mean_of)
    high, low = split(centered * centered)
    spread = dot(jnp.concatenate([high, low], 1), jnp.concatenate([mean_of, mean_of], 0))
    return centered * lax.rsqrt(spread + 1e-05) * norm_gain


def spread_mask(mask, group):
    n = mask.shape[1]
    pick = iota((n, LANES), 0) == 4 * group + iota((n, LANES), 1) // SLOT
    return dot(mask, jnp.where(pick, 1.0, 0.0).astype(BF16))


def put_projections(z, mask, wide_ref, put):
    scales = (1.0 / math.sqrt(SLOT), 1.0 / math.sqrt(LENGTH))
    for matrix in range(3):
        wide = HEADS * LANES
        out = dot(z, wide_ref[:, matrix * wide : (matrix + 1) * wide])
        for h in range(HEADS):
            one = out[:, h * LANES : (h + 1) * LANES]
            if matrix < 2:
                one = one * mask * scales[matrix]
            put(matrix, h, one)


def gate_kernel(z_ref, weight_ref, gate_ref, wide_ref):
    widen(weight_ref[...], wide_ref, 0)
    for block in range(z_ref.shape[0]):
        out = jax.nn.sigmoid(dot(z_ref[block], wide_ref[...]))
        for h in range(HEADS):
            gate_ref[h, block] = out[:, h * LANES : (h + 1) * LANES].astype(BF16)


def row_start_kernel(
    place_ref, xyz_ref, new_ref, sums_ref, pair_ref, mask_ref, radial_ref, gain_ref, weights_ref,
    x_ref, qkv_ref, z_ref, wide_ref,
):
    bins = 64
    for at in range(3):
        widen(weights_ref[at * CH : (at + 1) * CH, :], wide_ref, at * HEADS * LANES)
    far = [new_ref[place_ref[0] * 2 + half] for half in range(2)]
    far_xyz = [
        jnp.concatenate(
            [
                jnp.broadcast_to(part[:, g * 3 + c : g * 3 + c + 1], (8, LANES))
                for part in far
                for g in range(5)
            ],
            0,
        )
        for c in range(3)
    ]
    row = place_ref[2]
    lane = iota((1, LANES), 1)
    centers = (lane % bins).astype(F32) * (RADIAL_REACH / (bins - 1))
    width = bins / RADIAL_REACH
    table = radial_ref[...]
    blank = jnp.zeros_like(table)
    table = jnp.concatenate(
        [jnp.concatenate([table, blank], 1), jnp.concatenate([blank, table], 1)], 0
    )
    table_high, table_low = split(table)
    table = jnp.concatenate([table_high, table_low, table_high], 0)
    norm_gain = gain_ref[...]

    together = 2
    size = ROWS // 8 * COLS

    def some(step, carry):
        bases, rows = [], []
        for at in range(2 * together):
            n = (step * together * 2 + at) * 2
            off = [
                far_xyz[c]
                - jnp.where(
                    lane < bins,
                    xyz_ref[row, n & 7, (n >> 3) * 3 + c],
                    xyz_ref[row, (n + 1) & 7, ((n + 1) >> 3) * 3 + c],
                )
                for c in range(3)
            ]
            spacing = length_of(off[0] * off[0] + off[1] * off[1] + off[2] * off[2])
            away = (spacing - centers) * width
            bases.append(jnp.exp(-(away * away)))
        high, low = split(jnp.concatenate(bases, 0))
        added = dot(jnp.concatenate([high, high, low], 1), table)
        for i in range(4 * together):
            at = (i // 2) * COLS
            n = step * together * 4 + i
            part = added[at : at + COLS, (i % 2) * CH : (i % 2 + 1) * CH]
            rows.append((pair_ref[n].astype(F32) + part).astype(BF16))
            x_ref[n] = rows[-1]
        z = normed(jnp.concatenate(rows, 0), norm_gain).astype(BF16)
        for i in range(4 * together):
            at = (step * together + i // 4) * COLS
            half, at = at // size, at % size
            z_ref[half, pl.ds(pl.multiple_of(at, COLS), COLS), (i % 4) * CH : (i % 4 + 1) * CH] = z[
                i * COLS : (i + 1) * COLS
            ]
        return carry

    groups = ROWS // 4
    lax.fori_loop(0, groups // together, some, 0, unroll=True)
    for s in range(2):
        for h in range(HEADS):
            qkv_ref[h * 2 + s, 3 * size :] = sums_ref[...]
        mask = jnp.concatenate(
            [spread_mask(mask_ref[...], s * (groups // 2) + g) for g in range(groups // 2)], 0
        )

        def put(matrix, h, one):
            qkv_ref[h * 2 + s, matrix * size : (matrix + 1) * size] = one.astype(BF16)

        put_projections(z_ref[s], mask, wide_ref, put)


def gathered(parts_ref, which, g, across):
    count = parts_ref.shape[0]
    if across == COLS:
        at = (which * 5 + g) * across
        return jnp.concatenate([parts_ref[p, at : at + across, :] for p in range(count)], 0)
    size = parts_ref.shape[1] // 3
    return jnp.concatenate(
        [
            parts_ref[p, which * size : (which + 1) * size].astype(F32)[
                g * across : (g + 1) * across
            ]
            for p in range(count)
        ],
        0,
    ).astype(BF16)


def logits_kernel(across, core_ref, qkv_ref, own_ref, other_ref, q_ref, k_ref, sum_ref):
    for g in range(5):
        q_ref[:, g * LANES : (g + 1) * LANES] = gathered(qkv_ref, 0, g, across)
        k_ref[:, g * LANES : (g + 1) * LANES] = gathered(qkv_ref, 1, g, across)
    rows = 128
    for m in range(LENGTH // rows):
        sum_ref[m * rows : (m + 1) * rows, :] = lax.dot_general(
            q_ref[m * rows : (m + 1) * rows, :],
            k_ref[...],
            (((1,), (1,)), ((), ())),
            preferred_element_type=F32,
        )
    core = core_ref[0]
    own_ref[...] = sum_ref[pl.ds(pl.multiple_of(core * HALF, HALF), HALF), :]
    other_ref[...] = sum_ref[pl.ds(pl.multiple_of((1 - core) * HALF, HALF), HALF), :].astype(BF16)


def turned_dot(a, b):
    return sum(
        lax.dot_general(a, part, (((1,), (1,)), ((), ())), preferred_element_type=F32)
        for part in split3(b)
    )


def places_kernel(new_ref, out_ref):
    flat = new_ref[...].reshape(LANES, LANES)
    sides = []
    for g in range(5):
        pick = (iota((8, LANES), 1) == iota((8, LANES), 0) + 3 * g) & (iota((8, LANES), 0) < 3)
        sides.append(turned_dot(jnp.where(pick, 1.0, 0.0).astype(BF16), flat))
    parts = jnp.concatenate(split3(jnp.concatenate(sides, 1)), 0)
    at, token = iota((LENGTH, LENGTH), 0), iota((LENGTH, LENGTH), 1)
    target = (at & 127) // 8 * ROWS + at // LANES * 8 + (at & 7)
    moved = dot(parts, jnp.where(target == token, 1.0, 0.0).astype(BF16))
    out_ref[...] = moved[:8] + moved[8:16] + moved[16:]


def bias_kernel(place_ref, weight_ref, far_ref, out_ref):
    bins = 64
    far = far_ref[...]
    pick = iota((BLOCK, LENGTH), 1) == iota((BLOCK, LENGTH), 0) + place_ref[1]
    near = turned_dot(jnp.where(pick, 1.0, 0.0).astype(BF16), far)
    square = jnp.zeros((BLOCK, LENGTH), F32)
    for c in range(3):
        off = near[:, c : c + 1] - far[c : c + 1, :]
        square = square + off * off
    width = bins / RADIAL_REACH
    spacing = length_of(square) * width

    def some(at, total):
        for u in range(8):
            b = at * 8 + u
            away = spacing - b.astype(F32) * (width * RADIAL_REACH / (bins - 1))
            total = total + weight_ref[b, place_ref[0]] * jnp.exp(-(away * away))
        return total

    out_ref[...] = lax.fori_loop(0, bins // 8, some, jnp.zeros((BLOCK, LENGTH), F32))


def softmax_kernel(parts_ref, bias_ref, out_ref):
    count = parts_ref.shape[0]
    logits = bias_ref[...]
    for p in range(count):
        logits = logits + parts_ref[p].astype(F32)
    scaled = jnp.exp(logits - jnp.max(logits, axis=-1, keepdims=True))
    weights = (scaled / jnp.sum(scaled, axis=-1, keepdims=True)).astype(BF16)
    for p in range(count):
        out_ref[p] = weights


def mix_kernel(across, core_ref, own_ref, other_ref, parts_ref, out_ref, a_ref, v_ref):
    core = core_ref[0]
    for ref, half in ((own_ref, core), (other_ref, 1 - core)):
        rows = jnp.concatenate([ref[m].astype(F32) for m in range(OWNERS)], 0)[:HALF]
        a_ref[pl.ds(pl.multiple_of(half * HALF, HALF), HALF), :] = rows.astype(BF16)
    for g in range(5):
        v_ref[:, g * LANES : (g + 1) * LANES] = gathered(parts_ref, 2, g, across)
    rows = 160
    for m in range(LENGTH // rows):
        mixed = dot(a_ref[m * rows : (m + 1) * rows, :], v_ref[...])
        for p in range(rows // across):
            pieces = [
                mixed[p * across : (p + 1) * across, g * LANES : (g + 1) * LANES]
                for g in range(5)
            ]
            spare = out_ref.shape[1] - 5 * across
            if spare:
                pieces.append(jnp.zeros((spare, LANES), F32))
            out_ref[m * (rows // across) + p] = jnp.concatenate(pieces, 0).astype(BF16)


def column_start_kernel(
    x_ref, gate_ref, mixed_ref, mask_ref, gain_ref, weights_ref,
    new_ref, qkv_ref, turned_ref, z_ref, wide_out_ref, wide_ref,
):
    widen_out(weights_ref[3 * CH :, :], wide_out_ref)
    for at in range(3):
        widen(weights_ref[at * CH : (at + 1) * CH, :], wide_ref, at * HEADS * LANES)
    norm_gain = gain_ref[...]
    for s in range(2):
        gated = jnp.concatenate(
            [
                (gate_ref[h, s].astype(F32) * mixed_ref[h * 2 + s].astype(F32)).astype(BF16)
                for h in range(HEADS)
            ],
            1,
        )
        update = dot(gated, wide_out_ref[...])
        for g in range(5):
            rows = []
            for i in range(4):
                n = (s * 5 + g) * 4 + i
                part = update[g * COLS : (g + 1) * COLS, i * CH : (i + 1) * CH]
                rows.append((x_ref[n].astype(F32) + part).astype(BF16))
                new_ref[n] = rows[-1]
            z = normed(jnp.concatenate(rows, 0), norm_gain)
            first = (s * 5 + g) * 4 * COLS
            z_ref[first : first + 4 * COLS, :] = z
    for chunk in range(4):
        pieces, masks = [], []
        for g in range(5):
            column = (chunk * 5 + g) * 4
            pieces.append(
                jnp.concatenate(
                    [z_ref[pl.ds(column + i, ROWS, stride=COLS), :] for i in range(4)], 1
                )
            )
            masks.append(spread_mask(mask_ref[...], chunk * 5 + g))

        size = qkv_ref.shape[1] // 3
        z = jnp.concatenate(pieces, 0)
        spare = size - z.shape[0]
        z = jnp.concatenate([z, jnp.zeros((spare, z.shape[1]), F32)], 0).astype(BF16)
        turned_ref[chunk] = z
        mask = jnp.concatenate(masks + [jnp.zeros((spare, LANES), F32)], 0)

        def put(matrix, h, one):
            qkv_ref[h * 4 + chunk, matrix * size : (matrix + 1) * size] = one.astype(BF16)

        put_projections(z, mask, wide_ref, put)


def finish_kernel(x_ref, gate_ref, mixed_ref, wo_ref, out_ref, turned_ref, wide_out_ref):
    widen_out(wo_ref[...], wide_out_ref)
    for chunk in range(4):
        gated = jnp.concatenate(
            [
                gate_ref[h, chunk].astype(F32) * mixed_ref[h * 4 + chunk].astype(F32)
                for h in range(HEADS)
            ],
            1,
        ).astype(BF16)
        update = dot(gated, wide_out_ref[...])
        for g in range(5):
            for i in range(4):
                column = (chunk * 5 + g) * 4 + i
                turned_ref[pl.ds(column, ROWS, stride=COLS), :] = update[
                    g * ROWS : (g + 1) * ROWS, i * CH : (i + 1) * CH
                ]
    for n in range(ROWS):
        out_ref[n] = (x_ref[n].astype(F32) + turned_ref[n * COLS : (n + 1) * COLS, :]).astype(BF16)


def exchange(parts, axes):
    return lax.all_to_all(parts, axes, split_axis=0, concat_axis=0, tiled=True)


def swap_cores(x):
    return lax.ppermute(x, "core", [(0, 1), (1, 0)])


def column_tokens(mine, cols_n):
    device = lambda r, c: r * cols_n + c
    rows_n = 2 * cols_n
    ways = []
    for flip in (0, 1):
        pairs = [
            (device(r, c), device(2 * c + ((r % 2) ^ flip), r // 2))
            for r in range(rows_n)
            for c in range(cols_n)
        ]
        ways.append(lax.ppermute(mine, EVERYWHERE, pairs))
    return ways


def tied_attention(across, qkv, core, bias, sum_axes, pass_axes, beside):
    own, other = call(
        functools.partial(logits_kernel, across),
        (shape((HALF, LENGTH), F32), shape((HALF, LENGTH), BF16)),
        [SMEM, VMEM],
        [
            pltpu.VMEM((LENGTH, 5 * LANES), BF16),
            pltpu.VMEM((LENGTH, 5 * LANES), BF16),
            pltpu.VMEM((LENGTH, LENGTH), F32),
        ],
    )(core, qkv)
    parts = (own + swap_cores(other).astype(F32)).astype(BF16)
    parts = jnp.pad(parts, ((0, 16 * BLOCK - HALF), (0, 0))).reshape(16, BLOCK, LENGTH)
    parts, beside = lax.optimization_barrier((exchange(parts, sum_axes), beside))
    weights = call(softmax_kernel, shape((16, BLOCK, LENGTH), BF16), [VMEM] * 2)(
        parts, bias
    )
    own = exchange(weights, sum_axes)
    other = swap_cores(own)
    mixed = call(
        functools.partial(mix_kernel, across),
        shape((qkv.shape[0], 5 * across + 5 * across % 16, LANES), BF16),
        [SMEM, VMEM, VMEM, VMEM],
        [pltpu.VMEM((LENGTH, LENGTH), BF16), pltpu.VMEM((LENGTH, 5 * LANES), BF16)],
    )(core, own, other, qkv)
    return exchange(mixed, pass_axes), beside


def shards(
    pair, pair_mask, node_state, coords, neighbours, atom_type, type_table, node_query, node_key,
    node_value, edge_pair, edge_radial, node_out_w, coord_gain, radial_pair, row_gain, row_query,
    row_key, row_value, row_gate, row_out, row_bias, column_gain, column_query, column_key,
    column_value, column_gate, column_out, column_bias,
):
    rows_n, cols_n, channels = pair.shape
    row, col = lax.axis_index(("x", "y")), lax.axis_index(("z", "core"))
    core = lax.axis_index("core")[None].astype(jnp.int32)
    node_width = node_state.shape[1]
    onehot = (atom_type[:, None] == jnp.arange(type_table.shape[0], dtype=jnp.int32)[None, :])
    features = node_state + jnp.dot(onehot.astype(F32), type_table, precision=PRECISE)
    spare = LANES - node_width
    near = jnp.concatenate(
        [features, coords.T, jnp.zeros((rows_n, spare - coords.shape[0]), F32)], 1
    )
    ways = column_tokens(near, 8)
    place = jnp.stack([col * cols_n, (row % 2 == 0).astype(jnp.int32)]).astype(jnp.int32)
    remote = (pair, neighbours, node_query, node_key, node_value, edge_pair, edge_radial)
    small, sums = call(
        graph_kernel,
        (shape((128, 8, LANES), F32), shape((48, LANES), BF16)),
        [SMEM] * 2 + [VMEM] * 10,
        [pltpu.VMEM((ROWS, LANES), F32)] * 2,
        limit=60,
    )(place, coords, near, *ways, *remote)
    small, *weights = lax.optimization_barrier((small, row_query, row_key, row_value))
    weights = jnp.concatenate(weights, 0)
    small = exchange(small, EVERYWHERE)
    updated = call(merge_kernel, shape((16, 8, LANES), F32), [SMEM, VMEM])(coord_gain, small)
    place = jnp.stack([col, core[0], row]).astype(jnp.int32)

    groups = ROWS // 4
    projected = lambda count, size: [
        shape((ROWS, COLS, CH), BF16),
        shape((count, size, LANES), BF16),
    ]
    x, qkv, z = call(
        row_start_kernel,
        (*projected(8, 3 * 400 + 48), shape((2, 400, 4 * CH), BF16)),
        [SMEM] * 2 + [VMEM] * 7,
        [
            pltpu.VMEM((4 * CH, 3 * HEADS * LANES), BF16),
        ],
    )(
        place, updated, updated, sums, pair, pair_mask.T.astype(BF16), radial_pair, row_gain[None],
        weights,
    )

    qkv = exchange(qkv, ("z", "core"))
    all_xyz = call(places_kernel, shape((8, LENGTH), F32), [VMEM])(updated)
    new_coords = lax.dynamic_slice(all_xyz, (0, row * rows_n), (3, rows_n))
    new_state = call(
        node_kernel, shape((ROWS, node_width), F32), [SMEM] + [VMEM] * 4
    )(place, small, qkv, near, node_out_w)
    def gate(z, weight):
        return call(
            gate_kernel,
            shape((HEADS,) + z.shape[:2] + (LANES,), BF16),
            [VMEM] * 2,
            [pltpu.VMEM((4 * CH, HEADS * LANES), BF16)],
        )(z, weight)

    def bias(weight, head, owner):
        first = core[0] * HALF + jnp.minimum(owner, OWNERS - 1) * BLOCK
        return call(bias_kernel, shape((BLOCK, LENGTH), F32), [SMEM, SMEM, VMEM])(
            jnp.stack([head, first]).astype(jnp.int32), weight, all_xyz
        )

    row_biases = bias(row_bias, lax.axis_index("z"), row)
    column_biases = bias(column_bias, lax.axis_index("x"), lax.axis_index(("y", "z")))
    qkv, *weights = lax.optimization_barrier(
        (qkv, column_query, column_key, column_value, row_out)
    )
    weights = jnp.concatenate(weights, 0)
    mixed, (new_state, new_coords, row_gates) = tied_attention(
        COLS, qkv, core, row_biases, ("x", "y"), ("z", "core"),
        (new_state, new_coords, gate(z, row_gate)),
    )
    x, qkv, z = call(
        column_start_kernel,
        (*projected(16, 3 * 208), shape((4, 208, 4 * CH), BF16)),
        [VMEM] * 6,
        [
            pltpu.VMEM((ROWS * COLS, CH), F32),
            pltpu.VMEM((HEADS * LANES, 4 * CH), BF16),
            pltpu.VMEM((4 * CH, 3 * HEADS * LANES), BF16),
        ],
    )(
        x, row_gates, mixed, pair_mask.astype(BF16), column_gain[None], weights,
    )
    mixed, column_gates = tied_attention(
        ROWS, exchange(qkv, ("x", "y")), core, column_biases, ("y", "z"), ("x", "y"),
        gate(z, column_gate),
    )
    pair_out = call(
        finish_kernel,
        shape((ROWS, COLS, CH), BF16),
        [VMEM] * 4,
        [
            pltpu.VMEM((ROWS * COLS, CH), F32),
            pltpu.VMEM((HEADS * LANES, 4 * CH), BF16),
        ],
    )(x, column_gates, mixed, column_out)
    return (pair_out, new_state, new_coords)


def solution(mesh):
    cube = Mesh(mesh.devices.reshape(4, 4, 4, 2), EVERYWHERE)
    row, col = ("x", "y"), ("z", "core")
    placed = (
        P(row, col, None), P(row, col), P(row, None), P(None, row), P(row, None), P(row),
    ) + (P(),) * 23
    return jax.shard_map(
        shards,
        mesh=cube,
        in_specs=placed,
        out_specs=(P(row, col, None), P(row, None), P(None, row)),
        check_vma=False,
    )
```
